128 devices in a mesh: ctx: 8 (over z, core), dp: 16 (over y, x).
Axes of the slice: x: 4, y: 4, z: 4, core: 2. Of those that a mesh axis runs over, the one named last changes fastest.
Arguments:
- hidden_in: bfloat16 [16, 1024, 2048], P('dp', 'ctx'), may hold values from -6 to 6
- queries: bfloat16 [16, 1024, 1024], P('dp', 'ctx'), may hold values from -6 to 6
- key_vectors: bfloat16 [16, 1024, 1024], P('dp', 'ctx'), may hold values from -6 to 6
- value_rows: bfloat16 [16, 1024, 2048], P('dp', 'ctx'), may hold values from -6 to 6
- out_gate: bfloat16 [16, 1024, 2048], P('dp', 'ctx'), may hold values from -6 to 6
- beta_rate: float32 [16, 1024, 16], P('dp', 'ctx'), may hold values from 0.02 to 0.25
- log_decay: float32 [16, 1024, 16], P('dp', 'ctx'), may hold values from -1 to 0
- head_gain: float32 [128], replicated, may hold values from 0.1 to 1.9
- out_proj: bfloat16 [2048, 2048], replicated, may hold values from -0.125 to 0.125
- moe_gain: float32 [2048], replicated, may hold values from 0.1 to 1.9
- router: bfloat16 [2048, 32], replicated, may hold values from -0.125 to 0.125
- expert_ids: int32 [16, 1024, 10], P('dp', 'ctx'), may hold values from 0 to 31, all different within a row; in each aligned block of 128 rows (0 to 127, 128 to 255, ..., all dimensions but the last counted through in order) at most 80 rows name the same one
- expert_in: bfloat16 [32, 2, 2048, 512], P('dp'), may hold values from -0.125 to 0.125
- expert_down: bfloat16 [32, 512, 2048], P('dp'), may hold values from -0.75 to 0.75
Outputs:
- layer_out: bfloat16 [16, 1024, 2048], P('dp', 'ctx')
The draws below stay inside these ranges and needn't reach their ends.
Inputs may be any that keep to these rules, and one draw needn't show every extreme that they name: `expert_ids`: each position names 10 different experts. Within the rows of one device (aligned blocks of 128 positions of one sequence) no expert is named by more than 80 rows, a bound that some block reaches.
All inputs are finite; a program needn't handle non-finite values.
Results may differ from the reference program's by a relative error of at most 0.015.
Values may be sent and summed in bfloat16 or wider, within the bound.
A program may use at most 128 MiB of HBM per device.

```python
import math
import jax
import jax.numpy as jnp
import numpy as np
from jax import lax

D = 2048
HK = 8
HV = 16
DK = 128
DV = 128
FF = 512
TOP = 10
SPAN = 64
TOK_DEV = 128
SEQUENCE_LENGTH = 1024
BATCH_ROWS = 16
EXPERTS = 32
CAP = 80


def draw_log_decay(key, part):
    key = jax.random.fold_in(key, 7)
    random_keys = jax.random.split(key, 7)
    fast_share = 0.5
    forgetful = jax.random.bernoulli(random_keys[0], fast_share, (BATCH_ROWS, 1, HV))
    slow_speed = jnp.exp(jax.random.uniform(random_keys[1], (BATCH_ROWS, 1, HV), minval=math.log(0.05), maxval=math.log(0.3))) / SEQUENCE_LENGTH
    fast_speed = jnp.exp(jax.random.uniform(random_keys[2], (BATCH_ROWS, 1, HV), minval=math.log(1.0 / 50.0), maxval=math.log(1.0 / 25.0)))
    velocity = jnp.where(forgetful, fast_speed, slow_speed)
    block_count = SEQUENCE_LENGTH // SPAN
    block_factor = jnp.exp(jax.random.uniform(random_keys[3], (BATCH_ROWS, block_count, 1, 1), minval=math.log(0.5), maxval=math.log(2.0)))
    block_factor = jnp.broadcast_to(block_factor, (BATCH_ROWS, block_count, SPAN, 1)).reshape(BATCH_ROWS, SEQUENCE_LENGTH, 1)
    jaggedness = jax.random.uniform(random_keys[4], (BATCH_ROWS, SEQUENCE_LENGTH, HV), minval=0.5, maxval=1.5)
    spike_location = jax.random.randint(random_keys[5], (BATCH_ROWS, 2, 1), 0, SEQUENCE_LENGTH)
    hit_flags = jnp.any(jnp.arange(SEQUENCE_LENGTH)[None, None, :] == spike_location, axis=1)
    spike_penalty = jnp.log(jax.random.uniform(random_keys[6], (BATCH_ROWS, SEQUENCE_LENGTH, 1), minval=0.5, maxval=0.8))
    final_output = -velocity * block_factor * jaggedness + jnp.where(hit_flags[:, :, None], spike_penalty, 0.0)
    return final_output.astype(jnp.float32)


def block_scale(stream_key, dims, cuts, low, largest):
    def one(axis_at, parts):
        steps = jax.random.uniform(jax.random.fold_in(jax.random.fold_in(stream_key, 6), axis_at), (parts,), jnp.float32, low / len(cuts), largest / len(cuts))
        return jnp.repeat(jnp.exp(steps), dims[axis_at] // parts).reshape((-1,) + (1,) * (len(dims) - axis_at - 1))

    gain = one(*cuts[0])
    for cut in cuts[1:]:
        gain = gain * one(*cut)
    return gain


def assign_block(stream_key, own, number, rows, count, top, limit, lean):
    sequence = jax.random.permutation(stream_key, count)
    crowded, ordinary = shares(count, rows * top, limit, lean, True), shares(count, rows * top, limit, lean, False)
    places = jnp.arange(count)

    def named(tallies, rotation):
        used = int((tallies > 0).sum())
        fixed = max(1, used // 4)
        passed = fixed + (places - fixed + rotation * (used - fixed)) % max(1, count - fixed)
        return jnp.zeros((count,), jnp.int32).at[sequence[jnp.where(places < fixed, places, passed)]].set(jnp.asarray(tallies, jnp.int32))

    tallies = jnp.where(number % 4 == 0, named(crowded, number // 4), named(ordinary, number - number // 4 - 1))
    mixed = jax.random.permutation(jax.random.fold_in(own, 3), count)
    giver, taker = mixed[0:count // 2 * 2:2], mixed[1:count // 2 * 2:2]
    slack = jnp.minimum(tallies[giver] - 1, limit - tallies[taker]) // 2
    slack = jnp.where((giver == sequence[0]) | (taker == sequence[0]) | (tallies[taker] == 0), 0, jnp.maximum(slack, 0))
    passed = jax.random.randint(jax.random.fold_in(own, 4), (count // 2,), 0, 1 << 20) % (slack + 1)
    tallies = tallies.at[giver].add(-passed).at[taker].add(passed)
    items = jnp.searchsorted(jnp.cumsum(tallies), jnp.arange(rows * top), side="right").astype(jnp.int32)
    table = items.reshape(top, rows).T
    table = table[jax.random.permutation(jax.random.fold_in(own, 1), rows)]
    rotation = jax.random.randint(jax.random.fold_in(own, 2), (rows, 1), 0, top)
    return jnp.take_along_axis(table, (jnp.arange(top)[None, :] + rotation) % top, axis=1)


def shares(count, total, bound, slope, full):
    loads = [(1 << 20) // math.isqrt(rank ** slope) + 1 for rank in range(1, count + 1)]
    largest = bound if full else min(bound, max(-(-total // count), total * loads[0] // sum(loads)))
    least = 1 if total - largest >= count - 1 else 0
    given, spare = [largest] + [least] * (count - 1), total - largest - least * (count - 1)
    while spare > 0:
        candidates = [i for i in range(1, count) if given[i] < largest] or [i for i in range(1, count) if given[i] < bound]
        pool, remaining = sum([loads[i] for i in candidates]), spare
        for i in candidates:
            extra = min(bound - given[i], max(1, remaining * loads[i] // pool), spare)
            given[i] = given[i] + extra
            spare = spare - extra
    return np.array(given)


def normal_values(stream_key, dims, spread, most, shards=(), held_as=jnp.bfloat16):
    loudness = block_scale(stream_key, dims, shards, -0.22, 0.18) if shards else 1.0
    values = jax.random.normal(stream_key, dims, jnp.float32) * spread * loudness
    return jnp.minimum(jnp.maximum(values, -most), most).astype(held_as)


def setup_inputs(seed: int = 0) -> dict:
    streams_of = jax.random.split(jax.random.key(seed), 15)
    hidden_in = normal_values(streams_of[0], (BATCH_ROWS, SEQUENCE_LENGTH, D), 1.0, 6.0, ((0, 16), (1, 8)))
    queries = normal_values(streams_of[1], (BATCH_ROWS, SEQUENCE_LENGTH, HK * DK), 1.0, 6.0, ((0, 16), (1, 8)))
    key_vectors = normal_values(streams_of[2], (BATCH_ROWS, SEQUENCE_LENGTH, HK * DK), 1.0, 6.0, ((0, 16), (1, 8)))
    value_rows = normal_values(streams_of[3], (BATCH_ROWS, SEQUENCE_LENGTH, HV * DV), 1.0, 6.0, ((0, 16), (1, 8)))
    out_gate = normal_values(streams_of[4], (BATCH_ROWS, SEQUENCE_LENGTH, HV * DV), 1.0, 6.0, ((0, 16), (1, 8)))
    beta_rate = jnp.clip(0.02 + 0.23 * jax.random.uniform(streams_of[5], (BATCH_ROWS, SEQUENCE_LENGTH, HV), jnp.float32) ** block_scale(streams_of[5], (BATCH_ROWS, SEQUENCE_LENGTH, HV), ((0, 16), (1, 8)), -0.2, 0.2), 0.02, 0.25)
    log_decay = draw_log_decay(jax.random.fold_in(streams_of[14], 71), 0)
    head_gain = jnp.clip(1.0 + 0.18 * jax.random.normal(streams_of[7], (DV,), jnp.float32), 0.1, 1.9)
    out_proj = normal_values(streams_of[8], (HV * DV, D), (HV * DV) ** -0.5, 0.125)
    moe_gain = jnp.clip(1.0 + 0.18 * jax.random.normal(streams_of[9], (D,), jnp.float32), 0.1, 1.9)
    router = normal_values(streams_of[10], (D, EXPERTS), D ** -0.5, 0.125)
    expert_ids_keys = jax.random.split(jax.random.fold_in(streams_of[11], 1), BATCH_ROWS * SEQUENCE_LENGTH // TOK_DEV)
    expert_ids_turns = jax.random.permutation(jax.random.fold_in(streams_of[11], 3), BATCH_ROWS * SEQUENCE_LENGTH // TOK_DEV)
    expert_ids = jax.vmap(lambda own, number: assign_block(jax.random.fold_in(streams_of[11], 2), own, number, TOK_DEV, EXPERTS, TOP, CAP, 2))(expert_ids_keys, expert_ids_turns).reshape((BATCH_ROWS, SEQUENCE_LENGTH, TOP))
    expert_in = normal_values(streams_of[12], (EXPERTS, 2, D, FF), D ** -0.5, 0.125, ((0, 16),))
    expert_down = normal_values(streams_of[13], (EXPERTS, FF, D), (FF // 8) ** -0.5, 0.75, ((0, 16),))
    return {"hidden_in": hidden_in, "queries": queries, "key_vectors": key_vectors, "value_rows": value_rows, "out_gate": out_gate, "beta_rate": beta_rate, "log_decay": log_decay, "head_gain": head_gain, "out_proj": out_proj, "moe_gain": moe_gain, "router": router, "expert_ids": expert_ids, "expert_in": expert_in, "expert_down": expert_down}


def unit_rows(matrix):
    return matrix * lax.rsqrt(lax.optimization_barrier(jnp.sum(matrix * matrix, axis=-1, keepdims=True)) + 1e-06)

def delta_core(queries, key_vectors, value_rows, beta_rate, log_decay):
    highest = lax.Precision.HIGHEST
    group = HV // HK
    qnorm = jnp.repeat(unit_rows(queries.astype(jnp.float32).reshape(BATCH_ROWS, SEQUENCE_LENGTH, HK, DK)), group, axis=2)
    knorm = jnp.repeat(unit_rows(key_vectors.astype(jnp.float32).reshape(BATCH_ROWS, SEQUENCE_LENGTH, HK, DK)), group, axis=2)
    vnorm = value_rows.astype(jnp.float32).reshape(BATCH_ROWS, SEQUENCE_LENGTH, HV, DV)

    def advance(state, inputs):
        q_now, k_now, v_now, beta_now, decay_now = inputs
        state = state * jnp.exp(decay_now)[:, :, None, None]
        predicted = jnp.einsum('bhkv,bhk->bhv', state, k_now, precision=highest)
        state = state + jnp.einsum('bhk,bhv->bhkv', k_now * beta_now[:, :, None], v_now - predicted, precision=highest)
        output = jnp.einsum('bhkv,bhk->bhv', state, q_now, precision=highest)
        return (state, output)

    def moved(array):
        return jnp.moveaxis(array, 1, 0)
    initial = jnp.zeros((BATCH_ROWS, HV, DK, DV), jnp.float32)
    final_state, outputs = lax.scan(advance, initial, (moved(qnorm), moved(knorm), moved(vnorm), moved(beta_rate), moved(log_decay)))
    return jnp.moveaxis(outputs, 0, 1)

def reference(hidden_in, queries, key_vectors, value_rows, out_gate, beta_rate, log_decay, head_gain, out_proj, moe_gain, router, expert_ids, expert_in, expert_down):
    core = delta_core(queries, key_vectors, value_rows, beta_rate, log_decay)
    scale = lax.rsqrt(lax.optimization_barrier(jnp.mean(core * core, axis=-1, keepdims=True)) + 1e-06)
    gate_act = jax.nn.silu(out_gate.astype(jnp.float32).reshape(BATCH_ROWS, SEQUENCE_LENGTH, HV, DV))
    gated = (core * scale * head_gain * gate_act).astype(jnp.bfloat16).reshape(BATCH_ROWS * SEQUENCE_LENGTH, HV * DV)
    mixed = hidden_in.astype(jnp.float32).reshape(BATCH_ROWS * SEQUENCE_LENGTH, D) + jnp.dot(gated, out_proj, preferred_element_type=jnp.float32)
    normed = (mixed * lax.rsqrt(lax.optimization_barrier(jnp.mean(mixed * mixed, axis=-1, keepdims=True)) + 1e-06) * moe_gain).astype(jnp.bfloat16)
    logits = jnp.dot(normed, router, preferred_element_type=jnp.float32)
    chosen = expert_ids.reshape(BATCH_ROWS * SEQUENCE_LENGTH, TOP).astype(jnp.int32)
    picked = jnp.take_along_axis(logits, chosen, axis=1)
    sigmas = jax.nn.sigmoid(picked)
    gates = sigmas / lax.optimization_barrier(jnp.sum(sigmas, axis=1, keepdims=True))
    total = BATCH_ROWS * SEQUENCE_LENGTH
    blocks = total // TOK_DEV
    flat_expert = chosen.reshape(blocks, TOK_DEV * TOP)
    onehot = (flat_expert[:, :, None] == jnp.arange(EXPERTS, dtype=jnp.int32)[None, None, :]).astype(jnp.int32)
    before = jnp.cumsum(onehot, axis=1) - onehot
    slot = lax.optimization_barrier(jnp.sum(before * onehot, axis=2)).astype(jnp.int32)
    block_id = jnp.arange(blocks, dtype=jnp.int32)[:, None]
    token_id = (block_id * TOK_DEV + jnp.arange(TOK_DEV * TOP, dtype=jnp.int32)[None, :] // TOP).astype(jnp.int32)
    column = (block_id * CAP + slot).astype(jnp.int32)
    table_token = jnp.zeros((EXPERTS, blocks * CAP), jnp.int32).at[flat_expert, column].set(token_id)
    table_gate = jnp.zeros((EXPERTS, blocks * CAP), jnp.float32).at[flat_expert, column].set(gates.reshape(blocks, TOK_DEV * TOP))

    def expert_step(accum, pieces):
        weight_in, weight_down, tokens_of, gates_of = pieces
        rows = normed[tokens_of]
        gate_part = jnp.dot(rows, weight_in[0], preferred_element_type=jnp.float32)
        up_part = jnp.dot(rows, weight_in[1], preferred_element_type=jnp.float32)
        inner = (jax.nn.silu(gate_part) * up_part).astype(jnp.bfloat16)
        final_output = jnp.dot(inner, weight_down, preferred_element_type=jnp.float32).astype(jnp.bfloat16)
        accum = accum.at[tokens_of].add(gates_of[:, None] * final_output.astype(jnp.float32))
        return (accum, None)
    moe_sum, unused = lax.scan(expert_step, jnp.zeros((total, D), jnp.float32), (expert_in, expert_down, table_token, table_gate))
    return (mixed + moe_sum).astype(jnp.bfloat16).reshape(BATCH_ROWS, SEQUENCE_LENGTH, D)
```

```python
import functools

import jax
import jax.numpy as jnp
from jax import lax
from jax.experimental import pallas as pl
from jax.experimental.pallas import tpu as pltpu
from jax.sharding import PartitionSpec as P

DK = 128
DV = 128
SIDE = 4
HIGHEST = lax.Precision.HIGHEST
F32 = jnp.float32
BF16 = jnp.bfloat16


def dot_nn(a, b):
    return lax.dot_general(a, b, (((1,), (0,)), ((), ())), preferred_element_type=F32)


def dot_nt(a, b):
    return lax.dot_general(a, b, (((1,), (1,)), ((), ())), preferred_element_type=F32)


def dot_tn(a, b):
    return lax.dot_general(a, b, (((0,), (0,)), ((), ())), preferred_element_type=F32)


def unit_rows(matrix):
    return matrix * lax.rsqrt(jnp.sum(matrix * matrix, axis=-1, keepdims=True) + 1e-06)


HEADS_STEP = 4


def mixer_kernel(
    q_ref,
    k_ref,
    v_ref,
    z_ref,
    beta_ref,
    decay_ref,
    hidden_ref,
    head_gain_ref,
    moe_gain_ref,
    router_ref,
    ids_ref,
    proj_hbm,
    mixed_ref,
    normed_ref,
    proj_ref,
    cum_ref,
    add_ref,
    map_ref,
    growth_ref,
    core_add_ref,
    core_map_ref,
    state_in_ref,
    state_out_ref,
    acc_ref,
    proj_sem,
    send_sem,
    recv_sem,
):
    ctx = lax.axis_index("ctx")
    last = lax.axis_size("ctx") - 1
    tokens = q_ref.shape[0]
    heads = v_ref.shape[1] // DV
    groups = heads // HEADS_STEP
    barrier = pltpu.get_barrier_semaphore()

    for step in (1, last):
        pl.semaphore_signal(
            barrier, inc=1, device_id={"ctx": lax.rem(ctx + step, last + 1)}, device_id_type=pl.DeviceIdType.MESH
        )
    proj_copy = pltpu.make_async_copy(proj_hbm, proj_ref, proj_sem)
    proj_copy.start()

    rows = lax.broadcasted_iota(jnp.int32, (tokens, tokens), 0)
    cols = lax.broadcasted_iota(jnp.int32, (tokens, tokens), 1)
    lower = rows >= cols
    head_lane = lax.broadcasted_iota(jnp.int32, (tokens, heads), 1)
    cumul = lax.dot_general(
        lower.astype(F32), decay_ref[...], (((1,), (0,)), ((), ())),
        preferred_element_type=F32, precision=HIGHEST,
    )
    cum_ref[...] = cumul.T

    pl.semaphore_wait(barrier, 2)

    def chain_copy(group):
        part = pl.ds(group * HEADS_STEP, HEADS_STEP)
        return pltpu.make_async_remote_copy(
            src_ref=state_out_ref.at[part],
            dst_ref=state_in_ref.at[part],
            send_sem=send_sem.at[group],
            recv_sem=recv_sem.at[group],
            device_id={"ctx": lax.rem(ctx + 1, last + 1)},
            device_id_type=pl.DeviceIdType.MESH,
        )

    def local_group(group, carry):
        xs, lows, ratios, kns, qks, uses = [], [], [], [], [], []
        for pair in range(HEADS_STEP // 2):
            lanes = pl.ds(pl.multiple_of((group * (HEADS_STEP // 2) + pair) * DK, DK), DK)
            kn = unit_rows(k_ref[:, lanes].astype(F32))
            qn = unit_rows(q_ref[:, lanes].astype(F32))
            knb, qnb = kn.astype(BF16), qn.astype(BF16)
            kk, qk = dot_nt(knb, knb), dot_nt(qnb, knb)
            for half in range(2):
                head = group * HEADS_STEP + pair * 2 + half
                pick = head_lane == head
                beta = jnp.sum(jnp.where(pick, beta_ref[...], 0.0), axis=1, keepdims=True)
                cc = jnp.sum(jnp.where(pick, cumul, 0.0), axis=1, keepdims=True)
                cr = cum_ref[pl.ds(head, 1), :]
                ratio = jnp.where(lower, jnp.exp(jnp.minimum(cc - cr, 0.0)), 0.0)
                low = jnp.where(rows > cols, beta * ratio * kk, 0.0)
                xs.append(
                    jnp.where(rows == cols, 1.0, jnp.where(rows // 2 == cols // 2, -low, 0.0)).astype(BF16)
                )
                lows.append(low.astype(BF16))
                growth = jnp.exp(cc)
                end = cr[:, tokens - 1 : tokens]
                tail = (jnp.exp(end - cc) * kn).astype(BF16)
                vv = v_ref[:, pl.ds(pl.multiple_of(head * DV, DV), DV)].astype(F32)
                rhs = jnp.concatenate([beta * vv, (beta * growth) * kn], axis=1).astype(BF16)
                uses.append((head, rhs, tail, (qk * ratio).astype(BF16), growth * qn, jnp.exp(end)))
        size = 2
        while size < tokens:
            shift = size.bit_length()
            mask = ((rows >> shift) == (cols >> shift)) & ((rows >> (shift - 1)) != (cols >> (shift - 1)))
            zero = jnp.zeros((tokens, tokens), BF16)
            ys = [dot_nn(jnp.where(mask, low, zero), x).astype(BF16) for low, x in zip(lows, xs)]
            xs = [(x.astype(F32) - dot_nn(x, y)).astype(BF16) for x, y in zip(xs, ys)]
            size *= 2
        for x, (head, rhs, tail, inner, grown, end) in zip(xs, uses):
            uw = dot_nn(x, rhs).astype(BF16)
            both = dot_tn(tail, uw)
            add_ref[head] = both[:, :DV]
            map_ref[head] = both[:, DV:].astype(BF16)
            growth_ref[head] = jnp.broadcast_to(end, (8, DV))
            core = dot_nn(inner, uw)
            core_add_ref[head] = core[:, :DV]
            core_map_ref[head] = (grown - core[:, DV:]).astype(BF16)

            @pl.when(ctx == 0)
            def first_state():
                state_out_ref[head] = both[:, :DV].astype(BF16)
                state_in_ref[head] = jnp.zeros((DK, DV), BF16)

        @pl.when(ctx == 0)
        def first_send():
            chain_copy(group).start()

        return carry

    lax.fori_loop(0, groups, local_group, 0)
    proj_copy.wait()
    acc_ref[...] = hidden_ref[...].astype(F32)

    def finish_group(group, carry):
        @pl.when(ctx > 0)
        def receive():
            chain_copy(group).wait_recv()

        @pl.when((ctx > 0) & (ctx < last))
        def forward():
            for step in range(HEADS_STEP):
                head = group * HEADS_STEP + step
                state = state_in_ref[head]
                grown = growth_ref[head][0:1, :] * state.astype(F32)
                state_out_ref[head] = (grown - dot_nn(map_ref[head], state) + add_ref[head]).astype(BF16)
            chain_copy(group).start()

        pieces = []
        for step in range(HEADS_STEP):
            head = group * HEADS_STEP + step
            core = core_add_ref[head] + dot_nn(core_map_ref[head], state_in_ref[head])
            scale = lax.rsqrt(jnp.mean(core * core, axis=-1, keepdims=True) + 1e-06)
            zz = z_ref[:, pl.ds(pl.multiple_of(head * DV, DV), DV)].astype(F32)
            act = zz / (1.0 + jnp.exp(-zz))
            pieces.append((core * scale * head_gain_ref[...] * act).astype(BF16))
        gated = jnp.concatenate(pieces, axis=1)
        width = HEADS_STEP * DV
        acc_ref[...] += dot_nn(gated, proj_ref[pl.ds(pl.multiple_of(group * width, width), width), :])
        return carry

    lax.fori_loop(0, groups, finish_group, 0)
    mixed = acc_ref[...]
    mixed_ref[...] = mixed
    scale = lax.rsqrt(jnp.mean(mixed * mixed, axis=-1, keepdims=True) + 1e-06)
    normed = (mixed * scale * moe_gain_ref[...]).astype(BF16)
    logits = dot_nn(normed, router_ref[...])
    experts = router_ref.shape[1]
    lane = lax.broadcasted_iota(jnp.int32, (tokens, experts), 1)
    ids = ids_ref[...]
    chosen = lane == ids[:, 0:1]
    for k in range(1, ids.shape[1]):
        chosen = chosen | (lane == ids[:, k : k + 1])
    sigmas = jnp.where(chosen, 1.0 / (1.0 + jnp.exp(-logits)), 0.0)
    gates = sigmas / jnp.sum(sigmas, axis=1, keepdims=True)
    high = gates.astype(BF16)
    lows = (gates - high.astype(F32)).astype(BF16)
    width = mixed.shape[1]
    normed_ref[:, :width] = normed
    normed_ref[:, width:] = jnp.concatenate(
        [high, lows, jnp.zeros((tokens, 128 - 2 * experts), BF16)], axis=1
    )

    @pl.when(ctx < last)
    def drain():
        def one(group, carry):
            chain_copy(group).wait_send()
            return carry

        lax.fori_loop(0, groups, one, 0)


def mixer(q, k, v, z, beta, decay, hidden, head_gain, moe_gain, router, ids, proj):
    tokens, width = hidden.shape
    heads = v.shape[1] // DV
    vmem = pl.BlockSpec(memory_space=pltpu.VMEM)
    return pl.pallas_call(
        mixer_kernel,
        out_shape=(
            jax.ShapeDtypeStruct((tokens, width), F32),
            jax.ShapeDtypeStruct((tokens, width + 128), BF16),
        ),
        in_specs=[vmem] * 11 + [pl.BlockSpec(memory_space=pl.ANY)],
        out_specs=(vmem, vmem),
        scratch_shapes=[
            pltpu.VMEM(proj.shape, BF16),
            pltpu.VMEM((heads, tokens), F32),
            pltpu.VMEM((heads, DK, DV), F32),
            pltpu.VMEM((heads, DK, DV), BF16),
            pltpu.VMEM((heads, 8, DV), F32),
            pltpu.VMEM((heads, tokens, DV), F32),
            pltpu.VMEM((heads, tokens, DV), BF16),
            pltpu.VMEM((heads, DK, DV), BF16),
            pltpu.VMEM((heads, DK, DV), BF16),
            pltpu.VMEM((tokens, width), F32),
            pltpu.SemaphoreType.DMA,
            pltpu.SemaphoreType.DMA((heads // HEADS_STEP,)),
            pltpu.SemaphoreType.DMA((heads // HEADS_STEP,)),
        ],
        compiler_params=pltpu.CompilerParams(
            collective_id=0, has_side_effects=True, vmem_limit_bytes=40 * 1024 * 1024
        ),
    )(q, k, v, z, beta, decay, hidden, head_gain, moe_gain, router, ids, proj)


def moe_kernel(
    normed_ref,
    mixed_ref,
    win_hbm,
    wdown_hbm,
    out_ref,
    win_ref,
    wdown_ref,
    rows_ref,
    part_ref,
    far_ref,
    near_ref,
    inner_ref,
    w_sem,
    ag_send,
    ag_recv,
    rs_send,
    rs_recv,
):
    width = mixed_ref.shape[1]
    tokens = mixed_ref.shape[0]
    sub = tokens // 4
    local = win_ref.shape[0]
    experts = local * lax.axis_size("dp")
    dp = lax.axis_index("dp")
    row, col = dp // SIDE, lax.rem(dp, SIDE)

    def beside(dr, dc):
        return lax.rem(row + dr + SIDE, SIDE) * SIDE + lax.rem(col + dc + SIDE, SIDE)

    right, left, down, up = beside(0, 1), beside(0, -1), beside(1, 0), beside(-1, 0)
    first_axis = (right, left, down, up)
    second_axis = (down, up, right, left)

    barrier = pltpu.get_barrier_semaphore()
    for target in first_axis:
        pl.semaphore_signal(barrier, inc=1, device_id={"dp": target}, device_id_type=pl.DeviceIdType.MESH)
    in_copy = pltpu.make_async_copy(win_hbm, win_ref, w_sem.at[0])
    down_copy = pltpu.make_async_copy(wdown_hbm, wdown_ref, w_sem.at[1])
    for part in range(4):
        rows_ref[0, pl.ds(part * 4 * sub, sub), :] = normed_ref[pl.ds(part * sub, sub), :]
    pl.semaphore_wait(barrier, 4)

    def at(part, j):
        start = (part * 4 + j) * sub
        return pl.ds(start if isinstance(start, int) else pl.multiple_of(start, sub), sub)

    def remote(src, dst, send, recv, target):
        return pltpu.make_async_remote_copy(
            src_ref=src, dst_ref=dst, send_sem=send, recv_sem=recv,
            device_id={"dp": target}, device_id_type=pl.DeviceIdType.MESH,
        )

    def gather_copy(part, k, j, axis):
        nk, nj = (0, j + 1) if axis == 0 else (k + 1, j)
        slot = j if axis == 0 else 3 + k * 4 + j
        return remote(
            rows_ref.at[k, at(part, j)],
            rows_ref.at[nk, at(part, nj)],
            ag_send.at[part * 15 + slot],
            ag_recv.at[part * 15 + slot],
            first_axis[part] if axis == 0 else second_axis[part],
        )

    def gather_first(j):
        for part in range(4):
            gather_copy(part, 0, j - 1, 0).wait_recv()
            if j < 3:
                gather_copy(part, 0, j, 0).start()
        for part in range(4):
            gather_copy(part, 0, j, 1).start()

    def gather_second(k, j):
        for part in range(4):
            gather_copy(part, k - 1, j, 1).wait_recv()

            def onward():
                gather_copy(part, k, j, 1).start()

            if isinstance(k, int):
                if k < 3:
                    onward()
            else:
                pl.when(k < 3)(onward)

    def far_copy(part, k, j):
        return remote(
            part_ref.at[k, at(part, j)],
            far_ref.at[k - 1, at(part, j)],
            rs_send.at[part * 15 + (k - 1) * 4 + j],
            rs_recv.at[part * 15 + (k - 1) * 4 + j],
            second_axis[part],
        )

    def near_copy(part, j):
        return remote(
            part_ref.at[0, at(part, j)],
            near_ref.at[j - 1, pl.ds(part * sub, sub)],
            rs_send.at[part * 15 + 12 + j - 1],
            rs_recv.at[part * 15 + 12 + j - 1],
            first_axis[part],
        )

    def ffn_slice(k, s):
        e, half = s // 2, lax.rem(s, 2)
        quarter = win_ref.shape[3] // 2
        lanes = pl.ds(pl.multiple_of(half * quarter, quarter), quarter)
        x = rows_ref[k, :, :width]
        gate_part = dot_nn(x, win_ref[e, 0, :, lanes])
        up_part = dot_nn(x, win_ref[e, 1, :, lanes])
        extra = rows_ref[k, :, width:].astype(F32)
        lane = lax.broadcasted_iota(jnp.int32, extra.shape, 1)
        mine = dp * local + e
        pick = (lane == mine) | (lane == mine + experts)
        gate = jnp.sum(jnp.where(pick, extra, 0.0), axis=1, keepdims=True)
        inner = gate_part / (1.0 + jnp.exp(-gate_part)) * up_part * gate
        inner_ref[:, pl.ds(pl.multiple_of(s * quarter, quarter), quarter)] = inner.astype(BF16)

    def ffn_down(k):
        hidden = wdown_ref.shape[1]

        def tile(n, carry):
            lanes = pl.ds(pl.multiple_of(n * 256, 256), 256)
            total = dot_nn(inner_ref[:, :hidden], wdown_ref[0, :, lanes])
            for e in range(1, local):
                total += dot_nn(inner_ref[:, e * hidden : (e + 1) * hidden], wdown_ref[e, :, lanes])
            part_ref[k, :, lanes] = total.astype(BF16)
            return carry

        lax.fori_loop(0, width // 256, tile, 0)

    def far_step(k, j):
        for part in range(4):
            far_copy(part, k - 1, j).wait_recv()
            part_ref[k, at(part, j), :] = (
                part_ref[k, at(part, j), :].astype(F32) + far_ref[k - 2, at(part, j), :].astype(F32)
            ).astype(BF16)
            far_copy(part, k, j).start()

    for part in range(4):
        gather_copy(part, 0, 0, 0).start()
    for part in range(4):
        gather_copy(part, 0, 0, 1).start()
    in_copy.start()
    down_copy.start()
    gather_first(1)
    gather_second(1, 0)
    gather_first(2)
    gather_second(1, 1)
    gather_first(3)
    in_copy.wait()
    down_copy.wait()

    def step(i, carry):
        k, s = i // 4, lax.rem(i, 4)

        @pl.when((k == 0) & (s < 2))
        def early():
            gather_second(1, s + 2)

        @pl.when((k == 1) | (k == 2))
        def middle():
            gather_second(k + 1, s)

        @pl.when(k == 3)
        def late():
            far_step(2, lax.rem(s + 1, 4))

        ffn_slice(k, s)

        @pl.when(s == 3)
        def last_slice():
            ffn_down(k)

            @pl.when(k == 1)
            def first_sums():
                for j in (1, 2, 3, 0):
                    for part in range(4):
                        far_copy(part, 1, j).start()

        return carry

    lax.fori_loop(0, 16, step, 0)

    def third(j, carry):
        far_step(3, lax.rem(j + 1, 4))
        return carry

    lax.fori_loop(0, 4, third, 0)
    for j in (1, 2, 3, 0):
        for part in range(4):
            far_copy(part, 3, j).wait_recv()
            total = part_ref[0, at(part, j), :].astype(F32) + far_ref[2, at(part, j), :].astype(F32)
            if j != 1:
                came = (j + 3) % 4
                near_copy(part, came).wait_recv()
                total = total + near_ref[came - 1, pl.ds(part * sub, sub), :].astype(F32)
            if j != 0:
                part_ref[0, at(part, j), :] = total.astype(BF16)
                near_copy(part, j).start()
            else:
                span = pl.ds(part * sub, sub)
                out_ref[span, :] = (mixed_ref[span, :] + total).astype(BF16)

    for part in range(4):
        for j in range(3):
            gather_copy(part, 0, j, 0).wait_send()
        for k in range(3):
            for j in range(4):
                gather_copy(part, k, j, 1).wait_send()
                far_copy(part, k + 1, j).wait_send()
        for j in range(1, 4):
            near_copy(part, j).wait_send()


def moe(normed, mixed, win, wdown):
    tokens, width = mixed.shape
    vmem = pl.BlockSpec(memory_space=pltpu.VMEM)
    anywhere = pl.BlockSpec(memory_space=pl.ANY)
    return pl.pallas_call(
        moe_kernel,
        out_shape=jax.ShapeDtypeStruct((tokens, width), BF16),
        in_specs=[vmem, vmem, anywhere, anywhere],
        out_specs=vmem,
        scratch_shapes=[
            pltpu.VMEM(win.shape, BF16),
            pltpu.VMEM(wdown.shape, BF16),
            pltpu.VMEM((4, 4 * tokens, normed.shape[1]), BF16),
            pltpu.VMEM((4, 4 * tokens, width), BF16),
            pltpu.VMEM((3, 4 * tokens, width), BF16),
            pltpu.VMEM((3, tokens, width), BF16),
            pltpu.VMEM((4 * tokens, win.shape[0] * win.shape[3]), BF16),
            pltpu.SemaphoreType.DMA((2,)),
            pltpu.SemaphoreType.DMA((60,)),
            pltpu.SemaphoreType.DMA((60,)),
            pltpu.SemaphoreType.DMA((60,)),
            pltpu.SemaphoreType.DMA((60,)),
        ],
        compiler_params=pltpu.CompilerParams(
            collective_id=1, has_side_effects=True, vmem_limit_bytes=58 * 1024 * 1024
        ),
    )(normed, mixed, win, wdown)


def per_device(
    hidden_in,
    queries,
    key_vectors,
    value_rows,
    out_gate,
    beta_rate,
    log_decay,
    head_gain,
    out_proj,
    moe_gain,
    router,
    expert_ids,
    expert_in,
    expert_down,
):
    mixed, normed = mixer(
        queries[0],
        key_vectors[0],
        value_rows[0],
        out_gate[0],
        beta_rate[0],
        log_decay[0],
        hidden_in[0],
        head_gain[None],
        moe_gain[None],
        router,
        expert_ids[0],
        out_proj,
    )
    return moe(normed, mixed, expert_in, expert_down)[None]


def solution(mesh):
    in_specs = (
        P("dp", "ctx", None),
        P("dp", "ctx", None),
        P("dp", "ctx", None),
        P("dp", "ctx", None),
        P("dp", "ctx", None),
        P("dp", "ctx", None),
        P("dp", "ctx", None),
        P(),
        P(),
        P(),
        P(),
        P("dp", "ctx", None),
        P("dp", None, None, None),
        P("dp", None, None),
    )
    out_specs = P("dp", "ctx", None)
    return jax.shard_map(
        per_device, mesh=mesh, in_specs=in_specs, out_specs=out_specs, check_vma=False
    )
```

```python
import jax
import jax.numpy as jnp
from jax import lax
from jax.experimental import pallas as pl
from jax.experimental.pallas import tpu as pltpu
from jax.sharding import PartitionSpec as P

DK = 128
DV = 128
SIDE = 4
HIGHEST = lax.Precision.HIGHEST
F32 = jnp.float32
BF16 = jnp.bfloat16


def dot_nn(a, b):
    return lax.dot_general(a, b, (((1,), (0,)), ((), ())), preferred_element_type=F32)


def dot_nt(a, b):
    return lax.dot_general(a, b, (((1,), (1,)), ((), ())), preferred_element_type=F32)


def dot_tn(a, b):
    return lax.dot_general(a, b, (((0,), (0,)), ((), ())), preferred_element_type=F32)


def unit_rows(matrix):
    return matrix * lax.rsqrt(jnp.sum(matrix * matrix, axis=-1, keepdims=True) + 1e-06)


HEADS_STEP = 4
UNITS = 8
MESH = pl.DeviceIdType.MESH


def layer_kernel(
    q_hbm,
    k_hbm,
    v_hbm,
    z_hbm,
    beta_hbm,
    decay_hbm,
    hidden_hbm,
    head_gain_hbm,
    moe_gain_hbm,
    router_hbm,
    ids_hbm,
    proj_hbm,
    win_hbm,
    wdown_hbm,
    out_ref,
    q_ref,
    k_ref,
    v_ref,
    z_ref,
    beta_ref,
    decay_ref,
    hidden_ref,
    head_gain_ref,
    moe_gain_ref,
    router_ref,
    ids_ref,
    proj_ref,
    win_ref,
    wdown_ref,
    far_in_ref,
    far_down_ref,
    cum_ref,
    add_ref,
    map_ref,
    growth_ref,
    core_add_ref,
    core_map_ref,
    state_in_ref,
    state_out_ref,
    acc_ref,
    rows_ref,
    part_ref,
    xsum_ref,
    ysum_ref,
    inner_ref,
    in_sem,
    chain_send,
    chain_recv,
    fetch_send,
    fetch_recv,
    ring_send,
    ring_recv,
    share_send,
    share_recv,
    gx_send,
    gx_recv,
    gy_send,
    gy_recv,
    sx_send,
    sx_recv,
    sy_send,
    sy_recv,
):
    ctx = lax.axis_index("ctx")
    shards = lax.axis_size("ctx")
    last = shards - 1
    dp = lax.axis_index("dp")
    row, col = dp // SIDE, lax.rem(dp, SIDE)
    tokens, width = hidden_ref.shape
    heads = v_ref.shape[1] // DV
    groups = heads // HEADS_STEP
    experts = router_ref.shape[0]
    local = experts // lax.axis_size("dp")
    half = tokens // 2

    def beside(dr, dc):
        return lax.rem(row + dr + SIDE, SIDE) * SIDE + lax.rem(col + dc + SIDE, SIDE)

    def along(step):
        return lax.rem(ctx + step + shards, shards)

    right, left, down, up = beside(0, 1), beside(0, -1), beside(1, 0), beside(-1, 0)
    partner = beside(0, 2)
    sibling = ctx + 1 - 2 * lax.rem(ctx, 2)

    barrier = pltpu.get_barrier_semaphore()
    for target in (right, left, down, up, partner):
        pl.semaphore_signal(barrier, inc=1, device_id={"dp": target}, device_id_type=MESH)
    for step in (1, -1, 2, -2):
        pl.semaphore_signal(barrier, inc=1, device_id={"ctx": along(step)}, device_id_type=MESH)

    loads = [
        pltpu.make_async_copy(src, dst, in_sem.at[n])
        for n, (src, dst) in enumerate(
            (
                (decay_hbm, decay_ref),
                (beta_hbm, beta_ref),
                (k_hbm, k_ref),
                (q_hbm, q_ref),
                (v_hbm, v_ref),
                (z_hbm, z_ref),
                (hidden_hbm, hidden_ref),
                (head_gain_hbm, head_gain_ref),
                (moe_gain_hbm, moe_gain_ref),
                (router_hbm, router_ref),
                (ids_hbm, ids_ref),
                (proj_hbm, proj_ref),
                (win_hbm, win_ref),
                (wdown_hbm, wdown_ref),
            )
        )
    ]
    for load in loads[:11]:
        load.start()

    in_span = win_hbm.shape[0] // (UNITS * shards)
    down_span = wdown_hbm.shape[0] // (UNITS * shards)

    def piece(owner, u):
        n = u * shards + owner
        return (
            pl.ds(pl.multiple_of(n * in_span, in_span), in_span),
            pl.ds(pl.multiple_of(n * down_span, down_span), down_span),
        )

    class Both:
        def __init__(self, src, owner, u, send, recv, slot, target):
            spans = piece(owner, u)
            self.copies = [
                pltpu.make_async_remote_copy(
                    src_ref=ref.at[span],
                    dst_ref=dst.at[span],
                    send_sem=send.at[slot * 2 + n],
                    recv_sem=recv.at[slot * 2 + n],
                    device_id=target,
                    device_id_type=MESH,
                )
                for n, (ref, dst, span) in enumerate(zip(src, (far_in_ref, far_down_ref), spans))
            ]

        def start(self):
            for copy in self.copies:
                copy.start()

        def wait_recv(self):
            for copy in self.copies:
                copy.wait_recv()

        def wait_send(self):
            for copy in self.copies:
                copy.wait_send()

    far = (far_in_ref, far_down_ref)

    def fetch(u):
        return Both((win_hbm, wdown_hbm), ctx, u, fetch_send, fetch_recv, u, {"dp": partner})

    def ring(lane, owner, u, target):
        return Both(far, owner, u, ring_send, ring_recv, lane * UNITS + u, {"ctx": target})

    def share(lane, owner, u):
        return Both(far, owner, u, share_send, share_recv, lane * UNITS + u, {"ctx": sibling})

    def own_piece(u):
        fetch(u).wait_recv()
        ring(0, ctx, u, along(2)).start()
        ring(1, ctx, u, along(-2)).start()
        share(0, ctx, u).start()

    def ring_piece(u):
        behind, ahead = along(-2), along(2)
        ring(0, behind, u, along(2)).wait_recv()
        if u % 2 == 0:
            ring(2, behind, u, along(2)).start()
        share(1, behind, u).start()
        ring(1, ahead, u, along(-2)).wait_recv()
        if u % 2 == 1:
            ring(2, ahead, u, along(-2)).start()
        share(2, ahead, u).start()

    def ring_piece_far(u):
        ring(2, along(4), u, along(2)).wait_recv()
        share(3, along(4), u).start()

    def share_recv_all(u):
        for lane, step in enumerate((0, -2, 2, 4)):
            share(lane, lax.rem(sibling + step + shards, shards), u).wait_recv()

    pl.semaphore_wait(barrier, 9)
    for u in range(UNITS):
        fetch(u).start()
    for load in loads[11:]:
        load.start()
    for load in loads[:5]:
        load.wait()

    rows = lax.broadcasted_iota(jnp.int32, (tokens, tokens), 0)
    cols = lax.broadcasted_iota(jnp.int32, (tokens, tokens), 1)
    lower = rows >= cols
    head_lane = lax.broadcasted_iota(jnp.int32, (tokens, heads), 1)
    cum_rows = lax.dot_general(
        decay_ref[...], (rows <= cols).astype(F32), (((1,), (0,)), ((), ())),
        preferred_element_type=F32, precision=HIGHEST,
    )
    cum_ref[...] = cum_rows
    cumul = cum_rows.T
    betas = beta_ref[...].T

    def chain_copy(group):
        part = pl.ds(group * HEADS_STEP, HEADS_STEP)
        return pltpu.make_async_remote_copy(
            src_ref=state_out_ref.at[part],
            dst_ref=state_in_ref.at[part],
            send_sem=chain_send.at[group],
            recv_sem=chain_recv.at[group],
            device_id={"ctx": along(1)},
            device_id_type=MESH,
        )

    def local_group(group):
        xs, lows, uses = [], [], []
        for pair in range(HEADS_STEP // 2):
            lanes = pl.ds(pl.multiple_of((group * (HEADS_STEP // 2) + pair) * DK, DK), DK)
            kn = unit_rows(k_ref[:, lanes].astype(F32))
            qn = unit_rows(q_ref[:, lanes].astype(F32))
            knb, qnb = kn.astype(BF16), qn.astype(BF16)
            kk, qk = dot_nt(knb, knb), dot_nt(qnb, knb)
            for other in range(2):
                head = group * HEADS_STEP + pair * 2 + other
                pick = head_lane == head
                beta = jnp.sum(jnp.where(pick, betas, 0.0), axis=1, keepdims=True)
                cc = jnp.sum(jnp.where(pick, cumul, 0.0), axis=1, keepdims=True)
                cr = cum_ref[pl.ds(head, 1), :]
                ratio = jnp.where(lower, jnp.exp(jnp.minimum(cc - cr, 0.0)), 0.0)
                low = jnp.where(rows > cols, beta * ratio * kk, 0.0)
                xs.append(
                    jnp.where(rows == cols, 1.0, jnp.where(rows // 2 == cols // 2, -low, 0.0)).astype(BF16)
                )
                lows.append(low.astype(BF16))
                growth = jnp.exp(cc)
                end = cr[:, tokens - 1 : tokens]
                tail = (jnp.exp(end - cc) * kn).astype(BF16)
                vv = v_ref[:, pl.ds(pl.multiple_of(head * DV, DV), DV)].astype(F32)
                rhs = jnp.concatenate([beta * vv, (beta * growth) * kn], axis=1).astype(BF16)
                uses.append((head, rhs, tail, (qk * ratio).astype(BF16), growth * qn, jnp.exp(end)))
        size = 2
        while size < tokens:
            shift = size.bit_length()
            mask = ((rows >> shift) == (cols >> shift)) & ((rows >> (shift - 1)) != (cols >> (shift - 1)))
            zero = jnp.zeros((tokens, tokens), BF16)
            ys = [dot_nn(jnp.where(mask, low, zero), x).astype(BF16) for low, x in zip(lows, xs)]
            xs = [(x.astype(F32) - dot_nn(x, y)).astype(BF16) for x, y in zip(xs, ys)]
            size *= 2
        for x, (head, rhs, tail, inner, grown, end) in zip(xs, uses):
            uw = dot_nn(x, rhs).astype(BF16)
            both = dot_tn(tail, uw)
            add_ref[head] = both[:, :DV]
            map_ref[head] = both[:, DV:].astype(BF16)
            growth_ref[head] = jnp.broadcast_to(end, (8, DV))
            core = dot_nn(inner, uw)
            core_add_ref[head] = core[:, :DV]
            core_map_ref[head] = (grown - core[:, DV:]).astype(BF16)

            @pl.when(ctx == 0)
            def first_state():
                state_out_ref[head] = both[:, :DV].astype(BF16)
                state_in_ref[head] = jnp.zeros((DK, DV), BF16)

        @pl.when(ctx == 0)
        def first_send():
            chain_copy(group).start()

    def finish_group(group):
        @pl.when(ctx > 0)
        def receive():
            chain_copy(group).wait_recv()

        @pl.when((ctx > 0) & (ctx < last))
        def forward():
            for step in range(HEADS_STEP):
                head = group * HEADS_STEP + step
                state = state_in_ref[head]
                grown = growth_ref[head][0:1, :] * state.astype(F32)
                state_out_ref[head] = (grown - dot_nn(map_ref[head], state) + add_ref[head]).astype(BF16)
            chain_copy(group).start()

        pieces = []
        for step in range(HEADS_STEP):
            head = group * HEADS_STEP + step
            core = core_add_ref[head] + dot_nn(core_map_ref[head], state_in_ref[head])
            scale = lax.rsqrt(jnp.mean(core * core, axis=-1, keepdims=True) + 1e-06)
            zz = z_ref[:, pl.ds(pl.multiple_of(head * DV, DV), DV)].astype(F32)
            act = zz / (1.0 + jnp.exp(-zz))
            pieces.append((core * scale * head_gain_ref[...] * act).astype(BF16))
        gated = jnp.concatenate(pieces, axis=1)
        span = HEADS_STEP * DV
        acc_ref[...] += dot_nn(gated, proj_ref[pl.ds(pl.multiple_of(group * span, span), span), :])

    def local_step(group, carry):
        local_group(group)

        @pl.when(group == 1)
        def weights_a():
            own_piece(0)

        @pl.when(group == 2)
        def weights_b():
            own_piece(1)

        @pl.when(group == 3)
        def weights_c():
            own_piece(2)
            ring_piece(0)

        return carry

    lax.fori_loop(0, groups, local_step, 0)
    for load in loads[5:12]:
        load.wait()
    acc_ref[...] = hidden_ref[...].astype(F32)

    def finish_step(group, carry):
        finish_group(group)

        @pl.when(group == 0)
        def weights_a():
            own_piece(3)

        @pl.when(group == 2)
        def weights_b():
            ring_piece(1)

        return carry

    lax.fori_loop(0, groups, finish_step, 0)
    mixed = acc_ref[...]
    scale = lax.rsqrt(jnp.mean(mixed * mixed, axis=-1, keepdims=True) + 1e-06)
    normed = (mixed * scale * moe_gain_ref[...]).astype(BF16)
    logits = dot_nt(router_ref[...], normed)
    place = lax.broadcasted_iota(jnp.int32, (experts, tokens), 0)
    chosen = place == ids_ref[0]
    for k in range(1, ids_ref.shape[0]):
        chosen = chosen | (place == ids_ref[k])
    sigmas = jnp.where(chosen, 1.0 / (1.0 + jnp.exp(-logits)), 0.0)
    gates = (sigmas / jnp.sum(sigmas, axis=0, keepdims=True)).T
    high = gates.astype(BF16)
    lows = (gates - high.astype(F32)).astype(BF16)

    def own(k):
        return 2 * k - (k + 2) // 3

    def cross(k):
        return 2 * k + 2 - k // 3

    def at(slot, part):
        return pl.ds(pl.multiple_of(slot * tokens + part * half, half), half)

    rows_ref[pl.ds(0, tokens), :width] = normed
    rows_ref[pl.ds(0, tokens), width:] = jnp.concatenate(
        [high, lows, jnp.zeros((tokens, 128 - 2 * experts), BF16)], axis=1
    )

    def remote(src, dst, send, recv, target):
        return pltpu.make_async_remote_copy(
            src_ref=src, dst_ref=dst, send_sem=send, recv_sem=recv, device_id={"dp": target}, device_id_type=MESH
        )

    def gather_y(part, k):
        n = part * 3 + k
        return remote(
            rows_ref.at[at(own(k), part)], rows_ref.at[at(own(k + 1), part)],
            gy_send.at[n], gy_recv.at[n], (down, up)[part],
        )

    def gather_x(part, k):
        n = part * 4 + k
        return remote(
            rows_ref.at[at(own(k), part)], rows_ref.at[at(cross(k), part)],
            gx_send.at[n], gx_recv.at[n], (right, left)[part],
        )

    def sum_x(part, k):
        n = part * 4 + k
        return remote(
            part_ref.at[at(cross(k), part)], xsum_ref.at[at(k, part)],
            sx_send.at[n], sx_recv.at[n], (left, right)[part],
        )

    def sum_y(part, k):
        n = part * 3 + k - 1
        return remote(
            part_ref.at[at(own(k), part)], ysum_ref.at[at(k - 1, part)],
            sy_send.at[n], sy_recv.at[n], (down, up)[part],
        )

    def send_rows(k):
        for part in range(2):
            if k < 3:
                gather_y(part, k).start()
            gather_x(part, k).start()

    def take_rows(k):
        for part in range(2):
            gather_y(part, k - 1).wait_recv()
        send_rows(k)

    def take_cross(k):
        for part in range(2):
            gather_x(part, k).wait_recv()

    def ffn(start, count, in_ref, down_ref, first, number, owner, add):
        block = pl.ds(start if isinstance(start, int) else pl.multiple_of(start, tokens), count)
        hidden = down_ref.shape[0] // local
        quarter = hidden // 2

        def up_tile(n, carry):
            e = first + n // 2
            lanes = pl.ds(pl.multiple_of(lax.rem(n, 2) * quarter, quarter), quarter)
            x = rows_ref[block, :width]
            base = e * 2 * width
            gate_part = dot_nn(x, in_ref[pl.ds(pl.multiple_of(base, width), width), lanes])
            up_part = dot_nn(x, in_ref[pl.ds(pl.multiple_of(base + width, width), width), lanes])
            extra = rows_ref[block, width:].astype(F32)
            lane = lax.broadcasted_iota(jnp.int32, extra.shape, 1)
            mine = owner * local + e
            gate = jnp.sum(jnp.where((lane == mine) | (lane == mine + experts), extra, 0.0), axis=1, keepdims=True)
            inner = gate_part / (1.0 + jnp.exp(-gate_part)) * up_part * gate
            inner_ref[pl.ds(0, count), pl.ds(pl.multiple_of(n * quarter, quarter), quarter)] = inner.astype(BF16)
            return carry

        lax.fori_loop(0, 2 * number, up_tile, 0)

        def down_tile(n, carry):
            lanes = pl.ds(pl.multiple_of(n * 256, 256), 256)
            total = dot_nn(
                inner_ref[pl.ds(0, count), : number * hidden],
                down_ref[pl.ds(first * hidden, number * hidden), lanes],
            )
            if add:
                total += part_ref[block, lanes].astype(F32)
            part_ref[block, lanes] = total.astype(BF16)
            return carry

        lax.fori_loop(0, width // 256, down_tile, 0)

    def near_experts(slot, count):
        ffn(slot * tokens, count * tokens, win_ref, wdown_ref, 0, local, dp, False)

    def far_expert(slot, count, e):
        ffn(slot * tokens, count * tokens, far_in_ref, far_down_ref, e, 1, partner, True)

    send_rows(0)
    own_piece(4)
    ring_piece_far(0)
    for load in loads[12:]:
        load.wait()
    near_experts(0, 1)
    own_piece(5)
    ring_piece(2)
    ring_piece_far(1)
    take_rows(1)
    take_cross(0)

    def near_step(n, carry):
        near_experts(1 + 2 * n, 2)

        @pl.when(n == 0)
        def weights_a():
            ring_piece(3)
            own_piece(6)
            ring_piece_far(2)
            take_rows(2)
            take_cross(1)
            own_piece(7)
            ring_piece(4)

        @pl.when(n == 1)
        def weights_b():
            ring_piece_far(3)
            take_rows(3)
            take_cross(2)
            ring_piece(5)

        return carry

    lax.fori_loop(0, 3, near_step, 0)
    ring_piece_far(4)
    for u in range(UNITS // 2):
        share_recv_all(u)

    def far_first(n, carry):
        far_expert(2 * n, 2, 0)

        @pl.when(n == 0)
        def weights_a():
            ring_piece_far(5)
            ring_piece(6)

        @pl.when(n == 1)
        def weights_b():
            ring_piece_far(6)
            ring_piece(7)

        @pl.when(n == 2)
        def tail_rows():
            take_cross(3)
            near_experts(7, 1)

        return carry

    lax.fori_loop(0, 4, far_first, 0)
    ring_piece_far(7)
    for u in range(UNITS // 2, UNITS):
        share_recv_all(u)

    def far_cross(n, carry):
        k = lax.rem(n + 1, 4)
        far_expert(cross(k), 1, 1)
        for part in range(2):
            sum_x(part, k).start()
        return carry

    lax.fori_loop(0, 4, far_cross, 0)

    def far_own(n, carry):
        k = lax.rem(n + 1, 4)
        far_expert(own(k), 1, 1)
        for part in range(2):
            sum_x(part, k).wait_recv()
            spot = at(own(k), part)
            part_total = part_ref[spot, :].astype(F32) + xsum_ref[at(k, part), :].astype(F32)

            @pl.when(n == 0)
            def begin():
                part_ref[spot, :] = part_total.astype(BF16)

            @pl.when(n > 0)
            def more():
                sum_y(part, n).wait_recv()
                total = part_total + ysum_ref[at(n - 1, part), :].astype(F32)

                @pl.when(n < 3)
                def keep():
                    part_ref[spot, :] = total.astype(BF16)

                @pl.when(n == 3)
                def finish():
                    span = pl.ds(part * half, half)
                    out_ref[span, :] = (acc_ref[span, :] + total).astype(BF16)

            @pl.when(n < 3)
            def onward():
                sum_y(part, n + 1).start()

        return carry

    lax.fori_loop(0, 4, far_own, 0)

    for part in range(2):
        for k in range(4):
            gather_x(part, k).wait_send()
            sum_x(part, k).wait_send()
        for k in range(3):
            gather_y(part, k).wait_send()
            sum_y(part, k + 1).wait_send()
    for u in range(UNITS):
        fetch(u).wait_send()
        ring(0, ctx, u, along(2)).wait_send()
        ring(1, ctx, u, along(-2)).wait_send()
        ring(2, along(-2) if u % 2 == 0 else along(2), u, along(2)).wait_send()
        for lane, step in enumerate((0, -2, 2, 4)):
            share(lane, along(step), u).wait_send()

    @pl.when(ctx < last)
    def drain():
        for group in range(groups):
            chain_copy(group).wait_send()


def layer(q, k, v, z, beta, decay, hidden, head_gain, moe_gain, router, ids, proj, win, wdown):
    tokens, width = hidden.shape
    heads = v.shape[1] // DV
    args = (q, k, v, z, beta, decay, hidden, head_gain, moe_gain, router, ids, proj, win, wdown)
    hbm = pl.BlockSpec(memory_space=pltpu.HBM)
    dma = pltpu.SemaphoreType.DMA
    return pl.pallas_call(
        layer_kernel,
        out_shape=jax.ShapeDtypeStruct((tokens, width), BF16),
        in_specs=[hbm] * len(args),
        out_specs=pl.BlockSpec(memory_space=pltpu.VMEM),
        scratch_shapes=[pltpu.VMEM(arg.shape, arg.dtype) for arg in args]
        + [
            pltpu.VMEM(win.shape, BF16),
            pltpu.VMEM(wdown.shape, BF16),
            pltpu.VMEM((heads, tokens), F32),
            pltpu.VMEM((heads, DK, DV), F32),
            pltpu.VMEM((heads, DK, DV), BF16),
            pltpu.VMEM((heads, 8, DV), F32),
            pltpu.VMEM((heads, tokens, DV), F32),
            pltpu.VMEM((heads, tokens, DV), BF16),
            pltpu.VMEM((heads, DK, DV), BF16),
            pltpu.VMEM((heads, DK, DV), BF16),
            pltpu.VMEM((tokens, width), F32),
            pltpu.VMEM((8 * tokens, width + 128), BF16),
            pltpu.VMEM((8 * tokens, width), BF16),
            pltpu.VMEM((4 * tokens, width), BF16),
            pltpu.VMEM((3 * tokens, width), BF16),
            pltpu.VMEM((2 * tokens, wdown.shape[0]), BF16),
            dma((len(args),)),
            dma((heads // HEADS_STEP,)),
            dma((heads // HEADS_STEP,)),
            dma((2 * UNITS,)),
            dma((2 * UNITS,)),
            dma((6 * UNITS,)),
            dma((6 * UNITS,)),
            dma((8 * UNITS,)),
            dma((8 * UNITS,)),
            dma((8,)),
            dma((8,)),
            dma((6,)),
            dma((6,)),
            dma((8,)),
            dma((8,)),
            dma((6,)),
            dma((6,)),
        ],
        compiler_params=pltpu.CompilerParams(
            collective_id=0, has_side_effects=True, vmem_limit_bytes=62 * 1024 * 1024
        ),
    )(*args)


def per_device(
    hidden_in,
    queries,
    key_vectors,
    value_rows,
    out_gate,
    beta_rate,
    log_decay,
    head_gain,
    out_proj,
    moe_gain,
    router,
    expert_ids,
    expert_in,
    expert_down,
):
    return layer(
        queries[0],
        key_vectors[0],
        value_rows[0],
        out_gate[0],
        beta_rate[0].T,
        log_decay[0].T,
        hidden_in[0],
        head_gain[None],
        moe_gain[None],
        router.T,
        expert_ids.transpose(2, 0, 1),
        out_proj,
        expert_in.reshape(-1, expert_in.shape[-1]),
        expert_down.reshape(-1, expert_down.shape[-1]),
    )[None]


def solution(mesh):
    in_specs = (
        P("dp", "ctx", None),
        P("dp", "ctx", None),
        P("dp", "ctx", None),
        P("dp", "ctx", None),
        P("dp", "ctx", None),
        P("dp", "ctx", None),
        P("dp", "ctx", None),
        P(),
        P(),
        P(),
        P(),
        P("dp", "ctx", None),
        P("dp", None, None, None),
        P("dp", None, None),
    )
    out_specs = P("dp", "ctx", None)
    return jax.shard_map(
        per_device, mesh=mesh, in_specs=in_specs, out_specs=out_specs, check_vma=False
    )
```

```python
import jax
import jax.numpy as jnp
from jax import lax
from jax.experimental import pallas as pl
from jax.experimental.pallas import tpu as pltpu
from jax.sharding import PartitionSpec as P

DK = 128
DV = 128
SIDE = 4
HIGHEST = lax.Precision.HIGHEST
F32 = jnp.float32
BF16 = jnp.bfloat16


def dot_nn(a, b):
    return lax.dot_general(a, b, (((1,), (0,)), ((), ())), preferred_element_type=F32)


def dot_nt(a, b):
    return lax.dot_general(a, b, (((1,), (1,)), ((), ())), preferred_element_type=F32)


def dot_tn(a, b):
    return lax.dot_general(a, b, (((0,), (0,)), ((), ())), preferred_element_type=F32)


def unit_rows(matrix):
    return matrix * lax.rsqrt(jnp.sum(matrix * matrix, axis=-1, keepdims=True) + 1e-06)


HEADS_STEP = 4
UNITS = 8
MESH = pl.DeviceIdType.MESH


def layer_kernel(
    q_hbm,
    k_hbm,
    v_hbm,
    z_hbm,
    beta_hbm,
    decay_hbm,
    hidden_hbm,
    head_gain_hbm,
    moe_gain_hbm,
    router_hbm,
    ids_hbm,
    proj_hbm,
    win_hbm,
    wdown_hbm,
    out_ref,
    q_ref,
    k_ref,
    v_ref,
    z_ref,
    beta_ref,
    decay_ref,
    hidden_ref,
    head_gain_ref,
    moe_gain_ref,
    router_ref,
    ids_ref,
    proj_ref,
    win_ref,
    wdown_ref,
    far_in_ref,
    far_down_ref,
    cum_ref,
    add_ref,
    map_ref,
    growth_ref,
    core_add_ref,
    core_map_ref,
    state_in_ref,
    state_out_ref,
    acc_ref,
    rows_ref,
    part_ref,
    xsum_ref,
    ysum_ref,
    inner_ref,
    in_sem,
    chain_send,
    chain_recv,
    fetch_send,
    fetch_recv,
    ring_send,
    ring_recv,
    share_send,
    share_recv,
    gx_send,
    gx_recv,
    gy_send,
    gy_recv,
    sx_send,
    sx_recv,
    sy_send,
    sy_recv,
):
    ctx = lax.axis_index("ctx")
    shards = lax.axis_size("ctx")
    last = shards - 1
    dp = lax.axis_index("dp")
    row, col = dp // SIDE, lax.rem(dp, SIDE)
    tokens, width = hidden_ref.shape
    heads = v_ref.shape[1] // DV
    groups = heads // HEADS_STEP
    experts = router_ref.shape[0]
    local = experts // lax.axis_size("dp")
    half = tokens // 2

    def beside(dr, dc):
        return lax.rem(row + dr + SIDE, SIDE) * SIDE + lax.rem(col + dc + SIDE, SIDE)

    def along(step):
        return lax.rem(ctx + step + shards, shards)

    right, left, down, up = beside(0, 1), beside(0, -1), beside(1, 0), beside(-1, 0)
    partner = beside(0, 2)
    sibling = ctx + 1 - 2 * lax.rem(ctx, 2)

    barrier = pltpu.get_barrier_semaphore()
    for target in (right, left, down, up, partner):
        pl.semaphore_signal(barrier, inc=1, device_id={"dp": target}, device_id_type=MESH)
    for step in (1, -1, 2, -2):
        pl.semaphore_signal(barrier, inc=1, device_id={"ctx": along(step)}, device_id_type=MESH)

    loads = [
        pltpu.make_async_copy(src, dst, in_sem.at[n])
        for n, (src, dst) in enumerate(
            (
                (decay_hbm, decay_ref),
                (beta_hbm, beta_ref),
                (k_hbm, k_ref),
                (q_hbm, q_ref),
                (v_hbm, v_ref),
                (z_hbm, z_ref),
                (hidden_hbm, hidden_ref),
                (head_gain_hbm, head_gain_ref),
                (moe_gain_hbm, moe_gain_ref),
                (router_hbm, router_ref),
                (ids_hbm, ids_ref),
                (proj_hbm, proj_ref),
                (win_hbm, win_ref),
                (wdown_hbm, wdown_ref),
            )
        )
    ]
    for load in loads[:11]:
        load.start()

    in_span = win_hbm.shape[0] // (UNITS * shards)
    down_span = wdown_hbm.shape[0] // (UNITS * shards)

    def weight_spans(owner, u):
        n = u * shards + owner
        return (
            pl.ds(pl.multiple_of(n * in_span, in_span), in_span),
            pl.ds(pl.multiple_of(n * down_span, down_span), down_span),
        )

    class Both:
        def __init__(self, src, owner, u, send, recv, slot, target):
            spans = weight_spans(owner, u)
            self.copies = [
                pltpu.make_async_remote_copy(
                    src_ref=ref.at[span],
                    dst_ref=dst.at[span],
                    send_sem=send.at[slot * 2 + n],
                    recv_sem=recv.at[slot * 2 + n],
                    device_id=target,
                    device_id_type=MESH,
                )
                for n, (ref, dst, span) in enumerate(zip(src, (far_in_ref, far_down_ref), spans))
            ]

        def start(self):
            for copy in self.copies:
                copy.start()

        def wait_recv(self):
            for copy in self.copies:
                copy.wait_recv()

        def wait_send(self):
            for copy in self.copies:
                copy.wait_send()

    far = (far_in_ref, far_down_ref)

    def fetch(u):
        return Both((win_hbm, wdown_hbm), ctx, u, fetch_send, fetch_recv, u, {"dp": partner})

    def ring(lane, owner, u, target):
        return Both(far, owner, u, ring_send, ring_recv, lane * UNITS + u, {"ctx": target})

    def share(lane, owner, u):
        return Both(far, owner, u, share_send, share_recv, lane * UNITS + u, {"ctx": sibling})

    depth = ctx // 2
    top = depth == last // 2

    def own_piece(u, forward):
        fetch(u).wait_recv()
        ring(1, ctx, u, along(-2)).start()
        share(0, ctx, u).start()
        if forward:
            ring(0, ctx, u, along(2)).start()
        else:
            pl.when(top)(ring(0, ctx, u, along(2)).start)

    def piece_ahead(u):
        ahead = along(2)
        ring(1, ahead, u, along(-2)).wait_recv()

        @pl.when(lax.rem(u, 4) > 0)
        def onward():
            ring(2, ahead, u, along(-2)).start()

        share(2, ahead, u).start()

    def piece_behind(u):
        behind = along(-2)
        ring(0, behind, u, along(2)).wait_recv()

        @pl.when(lax.rem(u, 4) == 0)
        def onward():
            ring(2, behind, u, along(2)).start()

        share(1, behind, u).start()

    def piece_opposite(u):
        ring(2, along(4), u, along(2)).wait_recv()
        share(3, along(4), u).start()

    rounds = UNITS + 5

    def weights(since, until, forward=True):
        def weights_round(r, carry):
            @pl.when(r < UNITS)
            def one():
                own_piece(r, forward)

            @pl.when((r >= 2) & (r < UNITS + 2))
            def two():
                piece_ahead(r - 2)

            @pl.when((r >= 4) & (r < UNITS + 4))
            def three():
                piece_behind(r - 4)

            @pl.when(r >= 5)
            def four():
                piece_opposite(r - 5)

            return carry

        lax.fori_loop(since, until, weights_round, 0)

    before = jnp.maximum(depth, 1)
    after = jnp.minimum(depth + 2, 4)
    third = (2 * depth) // 3

    def share_recv_all(u):
        for lane, step in enumerate((0, -2, 2, 4)):
            share(lane, lax.rem(sibling + step + shards, shards), u).wait_recv()

    pl.semaphore_wait(barrier, 9)
    for u in range(UNITS):
        fetch(u).start()
    for load in loads[11:]:
        load.start()
    for load in loads[:5]:
        load.wait()

    rows = lax.broadcasted_iota(jnp.int32, (tokens, tokens), 0)
    cols = lax.broadcasted_iota(jnp.int32, (tokens, tokens), 1)
    lower = rows >= cols
    head_lane = lax.broadcasted_iota(jnp.int32, (tokens, heads), 1)
    cum_rows = lax.dot_general(
        decay_ref[...], (rows <= cols).astype(F32), (((1,), (0,)), ((), ())),
        preferred_element_type=F32, precision=HIGHEST,
    )
    cum_ref[...] = cum_rows
    cumul = cum_rows.T
    betas = beta_ref[...].T

    def chain_copy(group):
        part = pl.ds(group * HEADS_STEP, HEADS_STEP)
        return pltpu.make_async_remote_copy(
            src_ref=state_out_ref.at[part],
            dst_ref=state_in_ref.at[part],
            send_sem=chain_send.at[group],
            recv_sem=chain_recv.at[group],
            device_id={"ctx": along(1)},
            device_id_type=MESH,
        )

    def local_group(group):
        xs, lows, uses = [], [], []
        for pair in range(HEADS_STEP // 2):
            lanes = pl.ds(pl.multiple_of((group * (HEADS_STEP // 2) + pair) * DK, DK), DK)
            kn = unit_rows(k_ref[:, lanes].astype(F32))
            qn = unit_rows(q_ref[:, lanes].astype(F32))
            knb, qnb = kn.astype(BF16), qn.astype(BF16)
            kk, qk = dot_nt(knb, knb), dot_nt(qnb, knb)
            for other in range(2):
                head = group * HEADS_STEP + pair * 2 + other
                pick = head_lane == head
                beta = jnp.sum(jnp.where(pick, betas, 0.0), axis=1, keepdims=True)
                cc = jnp.sum(jnp.where(pick, cumul, 0.0), axis=1, keepdims=True)
                cr = cum_ref[pl.ds(head, 1), :]
                ratio = jnp.where(lower, jnp.exp(jnp.minimum(cc - cr, 0.0)), 0.0)
                low = jnp.where(rows > cols, beta * ratio * kk, 0.0)
                xs.append(
                    jnp.where(rows == cols, 1.0, jnp.where(rows // 2 == cols // 2, -low, 0.0)).astype(BF16)
                )
                lows.append(low.astype(BF16))
                growth = jnp.exp(cc)
                end = cr[:, tokens - 1 : tokens]
                tail = (jnp.exp(end - cc) * kn).astype(BF16)
                vv = v_ref[:, pl.ds(pl.multiple_of(head * DV, DV), DV)].astype(F32)
                rhs = jnp.concatenate([beta * vv, (beta * growth) * kn], axis=1).astype(BF16)
                uses.append((head, rhs, tail, (qk * ratio).astype(BF16), growth * qn, jnp.exp(end)))
        size = 2
        while size < tokens:
            shift = size.bit_length()
            mask = ((rows >> shift) == (cols >> shift)) & ((rows >> (shift - 1)) != (cols >> (shift - 1)))
            zero = jnp.zeros((tokens, tokens), BF16)
            ys = [dot_nn(jnp.where(mask, low, zero), x).astype(BF16) for low, x in zip(lows, xs)]
            xs = [(x.astype(F32) - dot_nn(x, y)).astype(BF16) for x, y in zip(xs, ys)]
            size *= 2
        for x, (head, rhs, tail, inner, grown, end) in zip(xs, uses):
            uw = dot_nn(x, rhs).astype(BF16)
            both = dot_tn(tail, uw)
            add_ref[head] = both[:, :DV]
            map_ref[head] = both[:, DV:].astype(BF16)
            growth_ref[head] = jnp.broadcast_to(end, (8, DV))
            core = dot_nn(inner, uw)
            core_add_ref[head] = core[:, :DV]
            core_map_ref[head] = (grown - core[:, DV:]).astype(BF16)

            @pl.when(ctx == 0)
            def first_state():
                state_out_ref[head] = both[:, :DV].astype(BF16)
                state_in_ref[head] = jnp.zeros((DK, DV), BF16)

        @pl.when(ctx == 0)
        def first_send():
            chain_copy(group).start()

    def finish_group(group):
        @pl.when(ctx > 0)
        def receive():
            chain_copy(group).wait_recv()

        @pl.when((ctx > 0) & (ctx < last))
        def forward():
            for step in range(HEADS_STEP):
                head = group * HEADS_STEP + step
                state = state_in_ref[head]
                grown = growth_ref[head][0:1, :] * state.astype(F32)
                state_out_ref[head] = (grown - dot_nn(map_ref[head], state) + add_ref[head]).astype(BF16)
            chain_copy(group).start()

        pieces = []
        for step in range(HEADS_STEP):
            head = group * HEADS_STEP + step
            core = core_add_ref[head] + dot_nn(core_map_ref[head], state_in_ref[head])
            scale = lax.rsqrt(jnp.mean(core * core, axis=-1, keepdims=True) + 1e-06)
            zz = z_ref[:, pl.ds(pl.multiple_of(head * DV, DV), DV)].astype(F32)
            act = zz / (1.0 + jnp.exp(-zz))
            pieces.append((core * scale * head_gain_ref[...] * act).astype(BF16))
        gated = jnp.concatenate(pieces, axis=1)
        span = HEADS_STEP * DV
        acc_ref[...] += dot_nn(gated, proj_ref[pl.ds(pl.multiple_of(group * span, span), span), :])

    def local_step(group, carry):
        local_group(group)

        return carry

    lax.fori_loop(0, groups, local_step, 0)
    weights(0, before, False)
    for load in loads[5:12]:
        load.wait()
    acc_ref[...] = hidden_ref[...].astype(F32)

    def finish_step(group, carry):
        finish_group(group)

        return carry

    lax.fori_loop(0, groups, finish_step, 0)

    def late_start(u, carry):
        ring(0, ctx, u, along(2)).start()
        return carry

    lax.fori_loop(0, jnp.where(top, 0, before), late_start, 0)
    mixed = acc_ref[...]
    scale = lax.rsqrt(jnp.mean(mixed * mixed, axis=-1, keepdims=True) + 1e-06)
    normed = (mixed * scale * moe_gain_ref[...]).astype(BF16)
    logits = dot_nt(router_ref[...], normed)
    place = lax.broadcasted_iota(jnp.int32, (experts, tokens), 0)
    chosen = place == ids_ref[0]
    for k in range(1, ids_ref.shape[0]):
        chosen = chosen | (place == ids_ref[k])
    sigmas = jnp.where(chosen, 1.0 / (1.0 + jnp.exp(-logits)), 0.0)
    gates = (sigmas / jnp.sum(sigmas, axis=0, keepdims=True)).T
    high = gates.astype(BF16)
    lows = (gates - high.astype(F32)).astype(BF16)

    quarter = half // 2

    def own(n):
        return 2 + n + 2 * (n // 2)

    def cross(n):
        return lax.rem(n + 4, 6)

    def at(slot, part, piece):
        return pl.ds(pl.multiple_of(slot * tokens + part * half + piece * quarter, quarter), quarter)

    home = pl.ds(7 * tokens, tokens)
    rows_ref[home, :width] = normed
    rows_ref[home, width:] = jnp.concatenate(
        [high, lows, jnp.zeros((tokens, 128 - 2 * experts), BF16)], axis=1
    )

    def remote(src, dst, send, recv, target):
        return pltpu.make_async_remote_copy(
            src_ref=src, dst_ref=dst, send_sem=send, recv_sem=recv, device_id={"dp": target}, device_id_type=MESH
        )

    def gather_y(part, k, piece):
        n = (part * 3 + k) * 2 + piece
        return remote(
            rows_ref.at[at(own(lax.rem(k + 3, 4)), part, piece)], rows_ref.at[at(own(k), part, piece)],
            gy_send.at[n], gy_recv.at[n], (down, up)[part],
        )

    def gather_x(part, k, piece):
        n = (part * 4 + k) * 2 + piece
        return remote(
            rows_ref.at[at(own(lax.rem(k + 3, 4)), part, piece)], rows_ref.at[at(cross(lax.rem(k + 3, 4)), part, piece)],
            gx_send.at[n], gx_recv.at[n], (right, left)[part],
        )

    def sum_x(part, n, piece):
        slot = (part * 4 + n) * 2 + piece
        return remote(
            part_ref.at[at(cross(n), part, piece)], xsum_ref.at[at(n, part, piece)],
            sx_send.at[slot], sx_recv.at[slot], (left, right)[part],
        )

    def sum_y(part, n, piece):
        slot = (part * 3 + n) * 2 + piece
        return remote(
            part_ref.at[at(own(n), part, piece)], ysum_ref.at[at(n, part, piece)],
            sy_send.at[slot], sy_recv.at[slot], (down, up)[part],
        )

    def send_rows(k, piece):
        for part in range(2):
            if isinstance(k, int):
                gather_y(part, k, piece).start()
            else:
                pl.when(k < 3)(gather_y(part, k, piece).start)
            gather_x(part, k, piece).start()

    def take_rows(k):
        for piece in range(2):
            for part in range(2):
                gather_y(part, k - 1, piece).wait_recv()
            send_rows(k, piece)

    def take_cross(k):
        for piece in range(2):
            for part in range(2):
                gather_x(part, k, piece).wait_recv()

    def ffn(start, count, in_ref, down_ref, first, number, owner, add):
        block = pl.ds(start if isinstance(start, int) else pl.multiple_of(start, tokens), count)
        hidden = down_ref.shape[0] // local

        def up_tile(n, carry):
            e = first + n
            x = rows_ref[block, :width]
            base = e * 2 * width
            base = base if isinstance(base, int) else pl.multiple_of(base, width)
            gate_part = dot_nn(x, in_ref[pl.ds(base, width), :])
            up_part = dot_nn(x, in_ref[pl.ds(base + width, width), :])
            extra = rows_ref[block, width:].astype(F32)
            lane = lax.broadcasted_iota(jnp.int32, extra.shape, 1)
            mine = owner * local + e
            gate = jnp.sum(jnp.where((lane == mine) | (lane == mine + experts), extra, 0.0), axis=1, keepdims=True)
            inner = gate_part / (1.0 + jnp.exp(-gate_part)) * up_part * gate
            lanes = pl.ds(0 if number == 1 else pl.multiple_of(n * hidden, hidden), hidden)
            inner_ref[pl.ds(0, count), lanes] = inner.astype(BF16)
            return carry

        if number == 1:
            up_tile(0, 0)
        else:
            lax.fori_loop(0, number, up_tile, 0)
        wide = width // 2

        def down_tile(n, carry):
            lanes = pl.ds(pl.multiple_of(n * wide, wide), wide)
            total = dot_nn(
                inner_ref[pl.ds(0, count), : number * hidden],
                down_ref[pl.ds(first * hidden, number * hidden), lanes],
            )
            if add:
                total += part_ref[block, lanes].astype(F32)
            part_ref[block, lanes] = total.astype(BF16)
            return carry

        lax.fori_loop(0, 2, down_tile, 0)

    def near_experts(slot, count):
        ffn(slot * tokens, count * tokens, win_ref, wdown_ref, 0, local, dp, False)

    def far_expert(slot, e):
        ffn(slot * tokens, 2 * tokens, far_in_ref, far_down_ref, e, 1, partner, True)

    send_rows(0, 0)
    send_rows(0, 1)
    weights(before, after)
    for load in loads[12:]:
        load.wait()
    near_experts(7, 1)
    weights(after, 4 + depth // 2)
    take_rows(1)
    take_cross(0)

    def near_step(n, carry):
        near_experts(1 + 2 * n, 2)

        @pl.when(n < 2)
        def more():
            take_rows(n + 2)
            weights(jnp.where(n == 0, 4 + depth // 2, 5 + third), 5 + n + third)
            take_cross(n + 1)

        return carry

    lax.fori_loop(0, 3, near_step, 0)
    weights(6 + third, 9)
    for u in range(UNITS // 2):
        share_recv_all(u)

    def far_first(n, carry):
        far_expert(lax.rem(4 + 2 * n, 8) - 2 * (n // 2) + 4 * (n // 2) - 4 * (n // 3), 0)

        @pl.when(n == 1)
        def tail_rows():
            take_cross(3)
            near_experts(0, 1)

        @pl.when(n < 3)
        def more():
            weights(9 + n, 10 + n)

        return carry

    lax.fori_loop(0, 4, far_first, 0)
    weights(12, rounds)
    for u in range(UNITS // 2, UNITS):
        share_recv_all(u)

    def far_cross(n, carry):
        far_expert(cross(2 * n), 1)
        for m in range(2):
            for piece in range(2):
                for part in range(2):
                    sum_x(part, 2 * n + m, piece).start()
        return carry

    lax.fori_loop(0, 2, far_cross, 0)

    def far_own(n, carry):
        far_expert(own(2 * n), 1)
        return carry

    lax.fori_loop(0, 2, far_own, 0)

    def collect(n, carry):
        for piece in range(2):
            for part in range(2):
                sum_x(part, n, piece).wait_recv()
                spot = at(own(n), part, piece)
                both = part_ref[spot, :].astype(F32) + xsum_ref[at(n, part, piece), :].astype(F32)

                @pl.when(n == 0)
                def begin():
                    part_ref[spot, :] = both.astype(BF16)

                @pl.when(n > 0)
                def more():
                    sum_y(part, n - 1, piece).wait_recv()
                    total = both + ysum_ref[at(n - 1, part, piece), :].astype(F32)

                    @pl.when(n < 3)
                    def keep():
                        part_ref[spot, :] = total.astype(BF16)

                    @pl.when(n == 3)
                    def finish():
                        span = pl.ds(part * half + piece * quarter, quarter)
                        out_ref[span, :] = (acc_ref[span, :] + total).astype(BF16)

                @pl.when(n < 3)
                def onward():
                    sum_y(part, n, piece).start()

        return carry

    lax.fori_loop(0, 4, collect, 0)

    for part in range(2):
        for piece in range(2):
            for k in range(4):
                gather_x(part, k, piece).wait_send()
                sum_x(part, k, piece).wait_send()
            for k in range(3):
                gather_y(part, k, piece).wait_send()
                sum_y(part, k, piece).wait_send()
    for u in range(UNITS):
        fetch(u).wait_send()
        ring(0, ctx, u, along(2)).wait_send()
        ring(1, ctx, u, along(-2)).wait_send()
        ring(2, along(-2) if u % 2 == 0 else along(2), u, along(2)).wait_send()
        for lane, step in enumerate((0, -2, 2, 4)):
            share(lane, along(step), u).wait_send()

    @pl.when(ctx < last)
    def drain():
        for group in range(groups):
            chain_copy(group).wait_send()


def layer(q, k, v, z, beta, decay, hidden, head_gain, moe_gain, router, ids, proj, win, wdown):
    tokens, width = hidden.shape
    heads = v.shape[1] // DV
    args = (q, k, v, z, beta, decay, hidden, head_gain, moe_gain, router, ids, proj, win, wdown)
    hbm = pl.BlockSpec(memory_space=pltpu.HBM)
    dma = pltpu.SemaphoreType.DMA
    return pl.pallas_call(
        layer_kernel,
        out_shape=jax.ShapeDtypeStruct((tokens, width), BF16),
        in_specs=[hbm] * len(args),
        out_specs=pl.BlockSpec(memory_space=pltpu.VMEM),
        scratch_shapes=[pltpu.VMEM(arg.shape, arg.dtype) for arg in args]
        + [
            pltpu.VMEM(win.shape, BF16),
            pltpu.VMEM(wdown.shape, BF16),
            pltpu.VMEM((heads, tokens), F32),
            pltpu.VMEM((heads, DK, DV), F32),
            pltpu.VMEM((heads, DK, DV), BF16),
            pltpu.VMEM((heads, 8, DV), F32),
            pltpu.VMEM((heads, tokens, DV), F32),
            pltpu.VMEM((heads, tokens, DV), BF16),
            pltpu.VMEM((heads, DK, DV), BF16),
            pltpu.VMEM((heads, DK, DV), BF16),
            pltpu.VMEM((tokens, width), F32),
            pltpu.VMEM((8 * tokens, width + 128), BF16),
            pltpu.VMEM((8 * tokens, width), BF16),
            pltpu.VMEM((4 * tokens, width), BF16),
            pltpu.VMEM((3 * tokens, width), BF16),
            pltpu.VMEM((2 * tokens, wdown.shape[0]), BF16),
            dma((len(args),)),
            dma((heads // HEADS_STEP,)),
            dma((heads // HEADS_STEP,)),
            dma((2 * UNITS,)),
            dma((2 * UNITS,)),
            dma((6 * UNITS,)),
            dma((6 * UNITS,)),
            dma((8 * UNITS,)),
            dma((8 * UNITS,)),
            dma((16,)),
            dma((16,)),
            dma((12,)),
            dma((12,)),
            dma((16,)),
            dma((16,)),
            dma((12,)),
            dma((12,)),
        ],
        compiler_params=pltpu.CompilerParams(
            collective_id=0, has_side_effects=True, vmem_limit_bytes=62 * 1024 * 1024
        ),
    )(*args)


def per_device(
    hidden_in,
    queries,
    key_vectors,
    value_rows,
    out_gate,
    beta_rate,
    log_decay,
    head_gain,
    out_proj,
    moe_gain,
    router,
    expert_ids,
    expert_in,
    expert_down,
):
    return layer(
        queries[0],
        key_vectors[0],
        value_rows[0],
        out_gate[0],
        beta_rate[0].T,
        log_decay[0].T,
        hidden_in[0],
        head_gain[None],
        moe_gain[None],
        router.T,
        expert_ids.transpose(2, 0, 1),
        out_proj,
        expert_in.reshape(-1, expert_in.shape[-1]),
        expert_down.reshape(-1, expert_down.shape[-1]),
    )[None]


def solution(mesh):
    in_specs = (
        P("dp", "ctx", None),
        P("dp", "ctx", None),
        P("dp", "ctx", None),
        P("dp", "ctx", None),
        P("dp", "ctx", None),
        P("dp", "ctx", None),
        P("dp", "ctx", None),
        P(),
        P(),
        P(),
        P(),
        P("dp", "ctx", None),
        P("dp", None, None, None),
        P("dp", None, None),
    )
    out_specs = P("dp", "ctx", None)
    return jax.shard_map(
        per_device, mesh=mesh, in_specs=in_specs, out_specs=out_specs, check_vma=False
    )
```

```python
import functools

import jax
import jax.numpy as jnp
from jax import lax
from jax.experimental import pallas as pl
from jax.experimental.pallas import tpu as pltpu
from jax.sharding import PartitionSpec as P

DK = 128
DV = 128
SIDE = 4
HIGHEST = lax.Precision.HIGHEST
F32 = jnp.float32
BF16 = jnp.bfloat16


def dot_nn(a, b):
    return lax.dot_general(a, b, (((1,), (0,)), ((), ())), preferred_element_type=F32)


def dot_nt(a, b):
    return lax.dot_general(a, b, (((1,), (1,)), ((), ())), preferred_element_type=F32)


def dot_tn(a, b):
    return lax.dot_general(a, b, (((0,), (0,)), ((), ())), preferred_element_type=F32)


def unit_rows(matrix):
    return matrix * lax.rsqrt(jnp.sum(matrix * matrix, axis=-1, keepdims=True) + 1e-06)


HEADS_STEP = 4
UNITS = 8
MESH = pl.DeviceIdType.MESH


def layer_kernel(
    q_hbm,
    k_hbm,
    v_hbm,
    z_hbm,
    beta_hbm,
    decay_hbm,
    hidden_hbm,
    head_gain_hbm,
    moe_gain_hbm,
    router_hbm,
    ids_hbm,
    proj_hbm,
    win_hbm,
    wdown_hbm,
    out_ref,
    q_ref,
    k_ref,
    v_ref,
    z_ref,
    beta_ref,
    decay_ref,
    hidden_ref,
    head_gain_ref,
    moe_gain_ref,
    router_ref,
    ids_ref,
    proj_ref,
    win_ref,
    wdown_ref,
    far_in_ref,
    far_down_ref,
    cum_ref,
    add_ref,
    map_ref,
    growth_ref,
    core_add_ref,
    core_map_ref,
    state_in_ref,
    state_out_ref,
    acc_ref,
    rows_ref,
    part_ref,
    xsum_ref,
    ysum_ref,
    inner_ref,
    in_sem,
    chain_send,
    chain_recv,
    fetch_send,
    fetch_recv,
    ring_send,
    ring_recv,
    share_send,
    share_recv,
    gx_send,
    gx_recv,
    gy_send,
    gy_recv,
    sx_send,
    sx_recv,
    sy_send,
    sy_recv,
):
    ctx = lax.axis_index("ctx")
    shards = lax.axis_size("ctx")
    last = shards - 1
    dp = lax.axis_index("dp")
    row, col = dp // SIDE, lax.rem(dp, SIDE)
    tokens, width = hidden_ref.shape
    heads = v_ref.shape[1] // DV
    groups = heads // HEADS_STEP
    experts = router_ref.shape[0]
    local = experts // lax.axis_size("dp")
    half = tokens // 2

    def beside(dr, dc):
        return lax.rem(row + dr + SIDE, SIDE) * SIDE + lax.rem(col + dc + SIDE, SIDE)

    def along(step):
        return lax.rem(ctx + step + shards, shards)

    right, left, down, up = beside(0, 1), beside(0, -1), beside(1, 0), beside(-1, 0)
    partner = beside(0, 2)
    sibling = ctx + 1 - 2 * lax.rem(ctx, 2)

    barrier = pltpu.get_barrier_semaphore()
    for target in (right, left, down, up, partner):
        pl.semaphore_signal(barrier, inc=1, device_id={"dp": target}, device_id_type=MESH)
    for step in (1, -1, 2, -2):
        pl.semaphore_signal(barrier, inc=1, device_id={"ctx": along(step)}, device_id_type=MESH)

    loads = [
        pltpu.make_async_copy(src, dst, in_sem.at[n])
        for n, (src, dst) in enumerate(
            (
                (decay_hbm, decay_ref),
                (beta_hbm, beta_ref),
                (k_hbm, k_ref),
                (q_hbm, q_ref),
                (v_hbm, v_ref),
                (z_hbm, z_ref),
                (hidden_hbm, hidden_ref),
                (head_gain_hbm, head_gain_ref),
                (moe_gain_hbm, moe_gain_ref),
                (router_hbm, router_ref),
                (ids_hbm, ids_ref),
                (proj_hbm, proj_ref),
                (win_hbm, win_ref),
                (wdown_hbm, wdown_ref),
            )
        )
    ]
    for load in loads[:11]:
        load.start()

    in_span = win_hbm.shape[0] // (UNITS * shards)
    down_span = wdown_hbm.shape[0] // (UNITS * shards)

    def weight_spans(owner, u):
        n = u * shards + owner
        return (
            pl.ds(pl.multiple_of(n * in_span, in_span), in_span),
            pl.ds(pl.multiple_of(n * down_span, down_span), down_span),
        )

    class Both:
        def __init__(self, src, owner, u, send, recv, slot, target):
            spans = weight_spans(owner, u)
            self.copies = [
                pltpu.make_async_remote_copy(
                    src_ref=ref.at[span],
                    dst_ref=dst.at[span],
                    send_sem=send.at[slot * 2 + n],
                    recv_sem=recv.at[slot * 2 + n],
                    device_id=target,
                    device_id_type=MESH,
                )
                for n, (ref, dst, span) in enumerate(zip(src, (far_in_ref, far_down_ref), spans))
            ]

        def start(self):
            for copy in self.copies:
                copy.start()

        def wait_recv(self):
            for copy in self.copies:
                copy.wait_recv()

        def wait_send(self):
            for copy in self.copies:
                copy.wait_send()

    far = (far_in_ref, far_down_ref)

    def fetch(u):
        return Both((win_hbm, wdown_hbm), ctx, u, fetch_send, fetch_recv, u, {"dp": partner})

    def ring(lane, owner, u, target):
        return Both(far, owner, u, ring_send, ring_recv, lane * UNITS + u, {"ctx": target})

    def share(lane, owner, u):
        return Both(far, owner, u, share_send, share_recv, lane * UNITS + u, {"ctx": sibling})

    depth = ctx // 2
    top = depth == last // 2

    def early_piece(u):
        fetch(u).wait_recv()
        ring(1, ctx, u, along(-2)).start()
        share(0, ctx, u).start()
        pl.when(top | (u < depth))(ring(0, ctx, u, along(2)).start)

    def own_piece(u):
        fetch(u).wait_recv()
        ring(1, ctx, u, along(-2)).start()
        share(0, ctx, u).start()
        ring(0, ctx, u, along(2)).start()

    def piece_ahead(u):
        ahead = along(2)
        ring(1, ahead, u, along(-2)).wait_recv()

        @pl.when(lax.rem(u, 4) > 0)
        def onward():
            ring(2, ahead, u, along(-2)).start()

        share(2, ahead, u).start()

    def piece_behind(u):
        behind = along(-2)
        ring(0, behind, u, along(2)).wait_recv()

        @pl.when(lax.rem(u, 4) == 0)
        def onward():
            ring(2, behind, u, along(2)).start()

        share(1, behind, u).start()

    def piece_opposite(u):
        ring(2, along(4), u, along(2)).wait_recv()
        share(3, along(4), u).start()

    kinds = (own_piece, piece_ahead, piece_behind, piece_opposite)

    def weights(since, until):
        for move, low, high in zip(kinds, since, until):
            if low is not high:

                def one(u, carry, move=move):
                    move(u)
                    return carry

                lax.fori_loop(low, high, one, 0)

    odd = (depth + 1) // 2
    early = (depth + 3, depth + 1, 0, 0)
    stages = (
        (depth + 5, jnp.minimum(depth + 3, 5), 2, 0),
        (UNITS, 4 + odd, 4, 1),
        (UNITS, 6 + odd, 6, 4),
        (UNITS, UNITS, 7, 5),
        (UNITS, UNITS, UNITS, 6),
        (UNITS, UNITS, UNITS, UNITS),
        (UNITS, UNITS, UNITS, UNITS),
        (UNITS, UNITS, UNITS, UNITS),
    )

    def pick(n, options):
        return tuple(
            functools.reduce(lambda other, m: jnp.where(n == m, options[m][kind], other), range(1, len(options)), options[0][kind])
            for kind in range(4)
        )

    def share_recv_all(u):
        for lane, step in enumerate((0, -2, 2, 4)):
            share(lane, lax.rem(sibling + step + shards, shards), u).wait_recv()

    pl.semaphore_wait(barrier, 9)
    for u in range(UNITS):
        fetch(u).start()
    for load in loads[11:]:
        load.start()
    for load in loads[:5]:
        load.wait()

    rows = lax.broadcasted_iota(jnp.int32, (tokens, tokens), 0)
    cols = lax.broadcasted_iota(jnp.int32, (tokens, tokens), 1)
    lower = rows >= cols
    head_lane = lax.broadcasted_iota(jnp.int32, (tokens, heads), 1)
    cum_rows = lax.dot_general(
        decay_ref[...], (rows <= cols).astype(F32), (((1,), (0,)), ((), ())),
        preferred_element_type=F32, precision=HIGHEST,
    )
    cum_ref[...] = cum_rows
    cumul = cum_rows.T
    betas = beta_ref[...].T

    def chain_copy(group):
        part = pl.ds(group * HEADS_STEP, HEADS_STEP)
        return pltpu.make_async_remote_copy(
            src_ref=state_out_ref.at[part],
            dst_ref=state_in_ref.at[part],
            send_sem=chain_send.at[group],
            recv_sem=chain_recv.at[group],
            device_id={"ctx": along(1)},
            device_id_type=MESH,
        )

    def local_group(group):
        xs, lows, uses = [], [], []
        for pair in range(HEADS_STEP // 2):
            lanes = pl.ds(pl.multiple_of((group * (HEADS_STEP // 2) + pair) * DK, DK), DK)
            kn = unit_rows(k_ref[:, lanes].astype(F32))
            qn = unit_rows(q_ref[:, lanes].astype(F32))
            knb, qnb = kn.astype(BF16), qn.astype(BF16)
            kk, qk = dot_nt(knb, knb), dot_nt(qnb, knb)
            for other in range(2):
                head = group * HEADS_STEP + pair * 2 + other
                pick = head_lane == head
                beta = jnp.sum(jnp.where(pick, betas, 0.0), axis=1, keepdims=True)
                cc = jnp.sum(jnp.where(pick, cumul, 0.0), axis=1, keepdims=True)
                cr = cum_ref[pl.ds(head, 1), :]
                ratio = jnp.where(lower, jnp.exp(jnp.minimum(cc - cr, 0.0)), 0.0)
                low = jnp.where(rows > cols, beta * ratio * kk, 0.0)
                xs.append(
                    jnp.where(rows == cols, 1.0, jnp.where(rows // 2 == cols // 2, -low, 0.0)).astype(BF16)
                )
                lows.append(low.astype(BF16))
                growth = jnp.exp(cc)
                end = cr[:, tokens - 1 : tokens]
                tail = (jnp.exp(end - cc) * kn).astype(BF16)
                vv = v_ref[:, pl.ds(pl.multiple_of(head * DV, DV), DV)].astype(F32)
                rhs = jnp.concatenate([beta * vv, (beta * growth) * kn], axis=1).astype(BF16)
                uses.append((head, rhs, tail, (qk * ratio).astype(BF16), growth * qn, jnp.exp(end)))
        size = 2
        while size < tokens:
            shift = size.bit_length()
            mask = ((rows >> shift) == (cols >> shift)) & ((rows >> (shift - 1)) != (cols >> (shift - 1)))
            zero = jnp.zeros((tokens, tokens), BF16)
            ys = [dot_nn(jnp.where(mask, low, zero), x).astype(BF16) for low, x in zip(lows, xs)]
            xs = [(x.astype(F32) - dot_nn(x, y)).astype(BF16) for x, y in zip(xs, ys)]
            size *= 2
        for x, (head, rhs, tail, inner, grown, end) in zip(xs, uses):
            uw = dot_nn(x, rhs).astype(BF16)
            both = dot_tn(tail, uw)
            add_ref[head] = both[:, :DV]
            map_ref[head] = both[:, DV:].astype(BF16)
            growth_ref[head] = jnp.broadcast_to(end, (8, DV))
            core = dot_nn(inner, uw)
            core_add_ref[head] = core[:, :DV]
            core_map_ref[head] = (grown - core[:, DV:]).astype(BF16)

            @pl.when(ctx == 0)
            def first_state():
                state_out_ref[head] = both[:, :DV].astype(BF16)
                state_in_ref[head] = jnp.zeros((DK, DV), BF16)

        @pl.when(ctx == 0)
        def first_send():
            chain_copy(group).start()

    def finish_group(group):
        @pl.when(ctx > 0)
        def receive():
            chain_copy(group).wait_recv()

        @pl.when((ctx > 0) & (ctx < last))
        def forward():
            for step in range(HEADS_STEP):
                head = group * HEADS_STEP + step
                state = state_in_ref[head]
                grown = growth_ref[head][0:1, :] * state.astype(F32)
                state_out_ref[head] = (grown - dot_nn(map_ref[head], state) + add_ref[head]).astype(BF16)
            chain_copy(group).start()

        pieces = []
        for step in range(HEADS_STEP):
            head = group * HEADS_STEP + step
            core = core_add_ref[head] + dot_nn(core_map_ref[head], state_in_ref[head])
            scale = lax.rsqrt(jnp.mean(core * core, axis=-1, keepdims=True) + 1e-06)
            zz = z_ref[:, pl.ds(pl.multiple_of(head * DV, DV), DV)].astype(F32)
            act = zz / (1.0 + jnp.exp(-zz))
            pieces.append((core * scale * head_gain_ref[...] * act).astype(BF16))
        gated = jnp.concatenate(pieces, axis=1)
        span = HEADS_STEP * DV
        acc_ref[...] += dot_nn(gated, proj_ref[pl.ds(pl.multiple_of(group * span, span), span), :])

    def local_step(group, carry):
        local_group(group)

        return carry

    lax.fori_loop(0, groups, local_step, 0)

    def early_own(u, carry):
        early_piece(u)
        return carry

    def early_ahead(u, carry):
        piece_ahead(u)
        return carry

    before = jnp.maximum(depth, 1)
    lax.fori_loop(0, before, early_own, 0)
    for load in loads[5:12]:
        load.wait()
    acc_ref[...] = hidden_ref[...].astype(F32)

    def finish_step(group, carry):
        finish_group(group)
        lax.fori_loop(
            jnp.where(group == 0, before, depth + 1 + group // 2), depth + 1 + (group + 1) // 2, early_own, 0
        )
        lax.fori_loop(
            jnp.where(group < 2, 0, depth),
            jnp.where(group == 0, 0, jnp.where(group < groups - 1, depth, depth + 1)),
            early_ahead,
            0,
        )
        return carry

    lax.fori_loop(0, groups, finish_step, 0)

    def late_start(u, carry):
        ring(0, ctx, u, along(2)).start()
        return carry

    lax.fori_loop(jnp.where(top, depth + 3, depth), depth + 3, late_start, 0)
    mixed = acc_ref[...]
    scale = lax.rsqrt(jnp.mean(mixed * mixed, axis=-1, keepdims=True) + 1e-06)
    normed = (mixed * scale * moe_gain_ref[...]).astype(BF16)
    logits = dot_nt(router_ref[...], normed)
    place = lax.broadcasted_iota(jnp.int32, (experts, tokens), 0)
    chosen = place == ids_ref[0]
    for k in range(1, ids_ref.shape[0]):
        chosen = chosen | (place == ids_ref[k])
    sigmas = jnp.where(chosen, 1.0 / (1.0 + jnp.exp(-logits)), 0.0)
    gates = (sigmas / jnp.sum(sigmas, axis=0, keepdims=True)).T
    high = gates.astype(BF16)
    lows = (gates - high.astype(F32)).astype(BF16)

    quarter = half // 2

    def own(n):
        return 2 + n + 2 * (n // 2)

    def cross(n):
        return lax.rem(n + 4, 6)

    def at(slot, part, piece):
        return pl.ds(pl.multiple_of(slot * tokens + part * half + piece * quarter, quarter), quarter)

    home = pl.ds(7 * tokens, tokens)
    rows_ref[home, :width] = normed
    rows_ref[home, width:] = jnp.concatenate(
        [high, lows, jnp.zeros((tokens, 128 - 2 * experts), BF16)], axis=1
    )

    def remote(src, dst, send, recv, target):
        return pltpu.make_async_remote_copy(
            src_ref=src, dst_ref=dst, send_sem=send, recv_sem=recv, device_id={"dp": target}, device_id_type=MESH
        )

    def gather_y(part, k, piece):
        n = (part * 3 + k) * 2 + piece
        return remote(
            rows_ref.at[at(own(lax.rem(k + 3, 4)), part, piece)], rows_ref.at[at(own(k), part, piece)],
            gy_send.at[n], gy_recv.at[n], (down, up)[part],
        )

    def gather_x(part, k, piece):
        n = (part * 4 + k) * 2 + piece
        return remote(
            rows_ref.at[at(own(lax.rem(k + 3, 4)), part, piece)], rows_ref.at[at(cross(lax.rem(k + 3, 4)), part, piece)],
            gx_send.at[n], gx_recv.at[n], (right, left)[part],
        )

    def sum_x(part, n, piece):
        slot = (part * 4 + n) * 2 + piece
        return remote(
            part_ref.at[at(cross(n), part, piece)], xsum_ref.at[at(n, part, piece)],
            sx_send.at[slot], sx_recv.at[slot], (left, right)[part],
        )

    def sum_y(part, n, piece):
        slot = (part * 3 + n) * 2 + piece
        return remote(
            part_ref.at[at(own(n), part, piece)], ysum_ref.at[at(n, part, piece)],
            sy_send.at[slot], sy_recv.at[slot], (down, up)[part],
        )

    def send_rows(k, piece):
        for part in range(2):
            if isinstance(k, int):
                gather_y(part, k, piece).start()
            else:
                pl.when(k < 3)(gather_y(part, k, piece).start)
            gather_x(part, k, piece).start()

    def take_rows(k):
        for piece in range(2):
            for part in range(2):
                gather_y(part, k - 1, piece).wait_recv()
            send_rows(k, piece)

    def take_cross(k):
        for piece in range(2):
            for part in range(2):
                gather_x(part, k, piece).wait_recv()

    def ffn(start, count, in_ref, down_ref, first, number, owner, add):
        block = pl.ds(start if isinstance(start, int) else pl.multiple_of(start, tokens), count)
        hidden = down_ref.shape[0] // local

        def up_tile(n, carry):
            e = first + n
            x = rows_ref[block, :width]
            base = e * 2 * width
            base = base if isinstance(base, int) else pl.multiple_of(base, width)
            gate_part = dot_nn(x, in_ref[pl.ds(base, width), :])
            up_part = dot_nn(x, in_ref[pl.ds(base + width, width), :])
            extra = rows_ref[block, width:].astype(F32)
            lane = lax.broadcasted_iota(jnp.int32, extra.shape, 1)
            mine = owner * local + e
            gate = jnp.sum(jnp.where((lane == mine) | (lane == mine + experts), extra, 0.0), axis=1, keepdims=True)
            inner = gate_part / (1.0 + jnp.exp(-gate_part)) * up_part * gate
            lanes = pl.ds(0 if number == 1 else pl.multiple_of(n * hidden, hidden), hidden)
            inner_ref[pl.ds(0, count), lanes] = inner.astype(BF16)
            return carry

        if number == 1:
            up_tile(0, 0)
        else:
            lax.fori_loop(0, number, up_tile, 0)
        wide = width // 2

        def down_tile(n, carry):
            lanes = pl.ds(pl.multiple_of(n * wide, wide), wide)
            total = dot_nn(
                inner_ref[pl.ds(0, count), : number * hidden],
                down_ref[pl.ds(first * hidden, number * hidden), lanes],
            )
            if add:
                total += part_ref[block, lanes].astype(F32)
            part_ref[block, lanes] = total.astype(BF16)
            return carry

        lax.fori_loop(0, 2, down_tile, 0)

    def near_experts(slot, count):
        ffn(slot * tokens, count * tokens, win_ref, wdown_ref, 0, local, dp, False)

    def far_expert(slot, e):
        ffn(slot * tokens, 2 * tokens, far_in_ref, far_down_ref, e, 1, partner, True)

    send_rows(0, 0)
    send_rows(0, 1)
    for load in loads[12:]:
        load.wait()
    near_experts(7, 1)
    weights(early, stages[0])
    take_rows(1)
    take_cross(0)

    def near_step(n, carry):
        near_experts(1 + 2 * n, 2)

        @pl.when(n < 2)
        def more():
            take_rows(n + 2)
            weights(pick(n, stages[0:2]), pick(n, stages[1:3]))
            take_cross(n + 1)

        return carry

    lax.fori_loop(0, 3, near_step, 0)
    weights(stages[2], stages[3])
    for u in range(UNITS // 2):
        share_recv_all(u)

    def far_first(n, carry):
        far_expert(lax.rem(4 + 2 * n, 8) - 2 * (n // 2) + 4 * (n // 2) - 4 * (n // 3), 0)

        @pl.when(n == 1)
        def tail_rows():
            take_cross(3)
            near_experts(0, 1)

        @pl.when(n < 3)
        def more():
            weights(pick(n, stages[3:6]), pick(n, stages[4:7]))

        return carry

    lax.fori_loop(0, 4, far_first, 0)
    weights(stages[6], stages[7])
    for u in range(UNITS // 2, UNITS):
        share_recv_all(u)

    def far_cross(n, carry):
        far_expert(cross(2 * n), 1)
        for m in range(2):
            for piece in range(2):
                for part in range(2):
                    sum_x(part, 2 * n + m, piece).start()
        return carry

    lax.fori_loop(0, 2, far_cross, 0)

    def far_own(n, carry):
        far_expert(own(2 * n), 1)
        return carry

    lax.fori_loop(0, 2, far_own, 0)

    def collect(n, carry):
        for piece in range(2):
            for part in range(2):
                sum_x(part, n, piece).wait_recv()
                spot = at(own(n), part, piece)
                both = part_ref[spot, :].astype(F32) + xsum_ref[at(n, part, piece), :].astype(F32)

                @pl.when(n == 0)
                def begin():
                    part_ref[spot, :] = both.astype(BF16)

                @pl.when(n > 0)
                def more():
                    sum_y(part, n - 1, piece).wait_recv()
                    total = both + ysum_ref[at(n - 1, part, piece), :].astype(F32)

                    @pl.when(n < 3)
                    def keep():
                        part_ref[spot, :] = total.astype(BF16)

                    @pl.when(n == 3)
                    def finish():
                        span = pl.ds(part * half + piece * quarter, quarter)
                        out_ref[span, :] = (acc_ref[span, :] + total).astype(BF16)

                @pl.when(n < 3)
                def onward():
                    sum_y(part, n, piece).start()

        return carry

    lax.fori_loop(0, 4, collect, 0)

    for part in range(2):
        for piece in range(2):
            for k in range(4):
                gather_x(part, k, piece).wait_send()
                sum_x(part, k, piece).wait_send()
            for k in range(3):
                gather_y(part, k, piece).wait_send()
                sum_y(part, k, piece).wait_send()
    for u in range(UNITS):
        fetch(u).wait_send()
        ring(0, ctx, u, along(2)).wait_send()
        ring(1, ctx, u, along(-2)).wait_send()
        ring(2, along(-2) if u % 2 == 0 else along(2), u, along(2)).wait_send()
        for lane, step in enumerate((0, -2, 2, 4)):
            share(lane, along(step), u).wait_send()

    @pl.when(ctx < last)
    def drain():
        for group in range(groups):
            chain_copy(group).wait_send()


def layer(q, k, v, z, beta, decay, hidden, head_gain, moe_gain, router, ids, proj, win, wdown):
    tokens, width = hidden.shape
    heads = v.shape[1] // DV
    args = (q, k, v, z, beta, decay, hidden, head_gain, moe_gain, router, ids, proj, win, wdown)
    hbm = pl.BlockSpec(memory_space=pltpu.HBM)
    dma = pltpu.SemaphoreType.DMA
    return pl.pallas_call(
        layer_kernel,
        out_shape=jax.ShapeDtypeStruct((tokens, width), BF16),
        in_specs=[hbm] * len(args),
        out_specs=pl.BlockSpec(memory_space=pltpu.VMEM),
        scratch_shapes=[pltpu.VMEM(arg.shape, arg.dtype) for arg in args]
        + [
            pltpu.VMEM(win.shape, BF16),
            pltpu.VMEM(wdown.shape, BF16),
            pltpu.VMEM((heads, tokens), F32),
            pltpu.VMEM((heads, DK, DV), F32),
            pltpu.VMEM((heads, DK, DV), BF16),
            pltpu.VMEM((heads, 8, DV), F32),
            pltpu.VMEM((heads, tokens, DV), F32),
            pltpu.VMEM((heads, tokens, DV), BF16),
            pltpu.VMEM((heads, DK, DV), BF16),
            pltpu.VMEM((heads, DK, DV), BF16),
            pltpu.VMEM((tokens, width), F32),
            pltpu.VMEM((8 * tokens, width + 128), BF16),
            pltpu.VMEM((8 * tokens, width), BF16),
            pltpu.VMEM((4 * tokens, width), BF16),
            pltpu.VMEM((3 * tokens, width), BF16),
            pltpu.VMEM((2 * tokens, wdown.shape[0]), BF16),
            dma((len(args),)),
            dma((heads // HEADS_STEP,)),
            dma((heads // HEADS_STEP,)),
            dma((2 * UNITS,)),
            dma((2 * UNITS,)),
            dma((6 * UNITS,)),
            dma((6 * UNITS,)),
            dma((8 * UNITS,)),
            dma((8 * UNITS,)),
            dma((16,)),
            dma((16,)),
            dma((12,)),
            dma((12,)),
            dma((16,)),
            dma((16,)),
            dma((12,)),
            dma((12,)),
        ],
        compiler_params=pltpu.CompilerParams(
            collective_id=0, has_side_effects=True, vmem_limit_bytes=62 * 1024 * 1024
        ),
    )(*args)


def per_device(
    hidden_in,
    queries,
    key_vectors,
    value_rows,
    out_gate,
    beta_rate,
    log_decay,
    head_gain,
    out_proj,
    moe_gain,
    router,
    expert_ids,
    expert_in,
    expert_down,
):
    return layer(
        queries[0],
        key_vectors[0],
        value_rows[0],
        out_gate[0],
        beta_rate[0].T,
        log_decay[0].T,
        hidden_in[0],
        head_gain[None],
        moe_gain[None],
        router.T,
        expert_ids.transpose(2, 0, 1),
        out_proj,
        expert_in.reshape(-1, expert_in.shape[-1]),
        expert_down.reshape(-1, expert_down.shape[-1]),
    )[None]


def solution(mesh):
    in_specs = (
        P("dp", "ctx", None),
        P("dp", "ctx", None),
        P("dp", "ctx", None),
        P("dp", "ctx", None),
        P("dp", "ctx", None),
        P("dp", "ctx", None),
        P("dp", "ctx", None),
        P(),
        P(),
        P(),
        P(),
        P("dp", "ctx", None),
        P("dp", None, None, None),
        P("dp", None, None),
    )
    out_specs = P("dp", "ctx", None)
    return jax.shard_map(
        per_device, mesh=mesh, in_specs=in_specs, out_specs=out_specs, check_vma=False
    )
```

```python
import functools

import jax
import jax.numpy as jnp
from jax import lax
from jax.experimental import pallas as pl
from jax.experimental.pallas import tpu as pltpu
from jax.sharding import PartitionSpec as P

DK = 128
DV = 128
SIDE = 4
HIGHEST = lax.Precision.HIGHEST
F32 = jnp.float32
BF16 = jnp.bfloat16


def dot_nn(a, b):
    return lax.dot_general(a, b, (((1,), (0,)), ((), ())), preferred_element_type=F32)


def dot_nt(a, b):
    return lax.dot_general(a, b, (((1,), (1,)), ((), ())), preferred_element_type=F32)


def dot_tn(a, b):
    return lax.dot_general(a, b, (((0,), (0,)), ((), ())), preferred_element_type=F32)


def unit_rows(matrix):
    return matrix * lax.rsqrt(jnp.sum(matrix * matrix, axis=-1, keepdims=True) + 1e-06)


HEADS_STEP = 4
UNITS = 8
MESH = pl.DeviceIdType.MESH


def layer_kernel(
    q_hbm,
    k_hbm,
    v_hbm,
    z_hbm,
    beta_hbm,
    decay_hbm,
    hidden_hbm,
    head_gain_hbm,
    moe_gain_hbm,
    router_hbm,
    ids_hbm,
    proj_hbm,
    win_hbm,
    wdown_hbm,
    out_ref,
    q_ref,
    k_ref,
    v_ref,
    z_ref,
    beta_ref,
    decay_ref,
    hidden_ref,
    head_gain_ref,
    moe_gain_ref,
    router_ref,
    ids_ref,
    proj_ref,
    win_ref,
    wdown_ref,
    far_in_ref,
    far_down_ref,
    cum_ref,
    add_ref,
    map_ref,
    growth_ref,
    core_add_ref,
    core_map_ref,
    state_in_ref,
    state_out_ref,
    acc_ref,
    rows_ref,
    part_ref,
    xsum_ref,
    ysum_ref,
    inner_ref,
    in_sem,
    chain_send,
    chain_recv,
    fetch_send,
    fetch_recv,
    ring_send,
    ring_recv,
    share_send,
    share_recv,
    gx_send,
    gx_recv,
    gy_send,
    gy_recv,
    sx_send,
    sx_recv,
    sy_send,
    sy_recv,
):
    ctx = lax.axis_index("ctx")
    shards = lax.axis_size("ctx")
    last = shards - 1
    dp = lax.axis_index("dp")
    row, col = dp // SIDE, lax.rem(dp, SIDE)
    tokens, width = hidden_ref.shape
    heads = v_ref.shape[1] // DV
    groups = heads // HEADS_STEP
    experts = router_ref.shape[0]
    local = experts // lax.axis_size("dp")
    half = tokens // 2

    def beside(dr, dc):
        return lax.rem(row + dr + SIDE, SIDE) * SIDE + lax.rem(col + dc + SIDE, SIDE)

    def along(step):
        return lax.rem(ctx + step + shards, shards)

    right, left, down, up = beside(0, 1), beside(0, -1), beside(1, 0), beside(-1, 0)
    partner = beside(0, 2)
    sibling = ctx + 1 - 2 * lax.rem(ctx, 2)

    barrier = pltpu.get_barrier_semaphore()
    for target in (right, left, down, up, partner):
        pl.semaphore_signal(barrier, inc=1, device_id={"dp": target}, device_id_type=MESH)
    for step in (1, -1, 2, -2):
        pl.semaphore_signal(barrier, inc=1, device_id={"ctx": along(step)}, device_id_type=MESH)

    loads = [
        pltpu.make_async_copy(src, dst, in_sem.at[n])
        for n, (src, dst) in enumerate(
            (
                (decay_hbm, decay_ref),
                (beta_hbm, beta_ref),
                (k_hbm, k_ref),
                (q_hbm, q_ref),
                (v_hbm, v_ref),
                (z_hbm, z_ref),
                (hidden_hbm, hidden_ref),
                (head_gain_hbm, head_gain_ref),
                (moe_gain_hbm, moe_gain_ref),
                (router_hbm, router_ref),
                (ids_hbm, ids_ref),
                (proj_hbm, proj_ref),
                (win_hbm, win_ref),
                (wdown_hbm, wdown_ref),
            )
        )
    ]
    for load in loads[:11]:
        load.start()

    in_span = win_hbm.shape[0] // (UNITS * shards)
    down_span = wdown_hbm.shape[0] // (UNITS * shards)

    def weight_spans(owner, u):
        n = u * shards + owner
        return (
            pl.ds(pl.multiple_of(n * in_span, in_span), in_span),
            pl.ds(pl.multiple_of(n * down_span, down_span), down_span),
        )

    class Both:
        def __init__(self, src, owner, u, send, recv, slot, target):
            spans = weight_spans(owner, u)
            self.copies = [
                pltpu.make_async_remote_copy(
                    src_ref=ref.at[span],
                    dst_ref=dst.at[span],
                    send_sem=send.at[slot * 2 + n],
                    recv_sem=recv.at[slot * 2 + n],
                    device_id=target,
                    device_id_type=MESH,
                )
                for n, (ref, dst, span) in enumerate(zip(src, (far_in_ref, far_down_ref), spans))
            ]

        def start(self):
            for copy in self.copies:
                copy.start()

        def wait_recv(self):
            for copy in self.copies:
                copy.wait_recv()

        def wait_send(self):
            for copy in self.copies:
                copy.wait_send()

    far = (far_in_ref, far_down_ref)

    def fetch(u):
        return Both((win_hbm, wdown_hbm), ctx, u, fetch_send, fetch_recv, u, {"dp": partner})

    def ring(lane, owner, u, target):
        return Both(far, owner, u, ring_send, ring_recv, lane * UNITS + u, {"ctx": target})

    def share(lane, owner, u):
        return Both(far, owner, u, share_send, share_recv, lane * UNITS + u, {"ctx": sibling})

    depth = ctx // 2
    top = depth == last // 2

    def early_piece(u):
        fetch(u).wait_recv()
        ring(1, ctx, u, along(-2)).start()
        share(0, ctx, u).start()
        pl.when(top | (u < depth))(ring(0, ctx, u, along(2)).start)

    def own_piece(u):
        fetch(u).wait_recv()
        ring(1, ctx, u, along(-2)).start()
        share(0, ctx, u).start()
        ring(0, ctx, u, along(2)).start()

    def piece_ahead(u):
        ahead = along(2)
        ring(1, ahead, u, along(-2)).wait_recv()

        @pl.when(lax.rem(u, 4) > 0)
        def onward():
            ring(2, ahead, u, along(-2)).start()

        share(2, ahead, u).start()

    def piece_behind(u):
        behind = along(-2)
        ring(0, behind, u, along(2)).wait_recv()

        @pl.when(lax.rem(u, 4) == 0)
        def onward():
            ring(2, behind, u, along(2)).start()

        share(1, behind, u).start()

    def piece_opposite(u):
        ring(2, along(4), u, along(2)).wait_recv()
        share(3, along(4), u).start()

    kinds = (own_piece, piece_ahead, piece_behind, piece_opposite)

    def weights(since, until):
        for move, low, high in zip(kinds, since, until):
            if low is not high:

                def one(u, carry, move=move):
                    move(u)
                    return carry

                lax.fori_loop(low, high, one, 0)

    odd = (depth + 1) // 2
    early = (depth + 3, depth + 1, 0, 0)
    stages = (
        (depth + 5, jnp.minimum(depth + 3, 5), 2, 0),
        (UNITS, 4 + odd, 4, 1),
        (UNITS, 6 + odd, 6, 4),
        (UNITS, UNITS, 7, 5),
        (UNITS, UNITS, UNITS, 6),
        (UNITS, UNITS, UNITS, UNITS),
        (UNITS, UNITS, UNITS, UNITS),
        (UNITS, UNITS, UNITS, UNITS),
    )

    def pick(n, options):
        return tuple(
            functools.reduce(lambda other, m: jnp.where(n == m, options[m][kind], other), range(1, len(options)), options[0][kind])
            for kind in range(4)
        )

    def share_recv_all(u):
        for lane, step in enumerate((0, -2, 2, 4)):
            share(lane, lax.rem(sibling + step + shards, shards), u).wait_recv()

    pl.semaphore_wait(barrier, 9)
    for u in range(UNITS):
        fetch(u).start()
    for load in loads[11:]:
        load.start()
    for load in loads[:5]:
        load.wait()

    rows = lax.broadcasted_iota(jnp.int32, (tokens, tokens), 0)
    cols = lax.broadcasted_iota(jnp.int32, (tokens, tokens), 1)
    lower = rows >= cols
    head_lane = lax.broadcasted_iota(jnp.int32, (tokens, heads), 1)
    cum_rows = lax.dot_general(
        decay_ref[...], (rows <= cols).astype(F32), (((1,), (0,)), ((), ())),
        preferred_element_type=F32, precision=HIGHEST,
    )
    cum_ref[...] = cum_rows
    cumul = cum_rows.T
    betas = beta_ref[...].T

    def chain_copy(group):
        part = pl.ds(group * HEADS_STEP, HEADS_STEP)
        return pltpu.make_async_remote_copy(
            src_ref=state_out_ref.at[part],
            dst_ref=state_in_ref.at[part],
            send_sem=chain_send.at[group],
            recv_sem=chain_recv.at[group],
            device_id={"ctx": along(1)},
            device_id_type=MESH,
        )

    def local_group(group):
        xs, lows, uses = [], [], []
        for pair in range(HEADS_STEP // 2):
            lanes = pl.ds(pl.multiple_of((group * (HEADS_STEP // 2) + pair) * DK, DK), DK)
            kn = unit_rows(k_ref[:, lanes].astype(F32))
            qn = unit_rows(q_ref[:, lanes].astype(F32))
            knb, qnb = kn.astype(BF16), qn.astype(BF16)
            kk, qk = dot_nt(knb, knb), dot_nt(qnb, knb)
            for other in range(2):
                head = group * HEADS_STEP + pair * 2 + other
                pick = head_lane == head
                beta = jnp.sum(jnp.where(pick, betas, 0.0), axis=1, keepdims=True)
                cc = jnp.sum(jnp.where(pick, cumul, 0.0), axis=1, keepdims=True)
                cr = cum_ref[pl.ds(head, 1), :]
                ratio = jnp.where(lower, jnp.exp(jnp.minimum(cc - cr, 0.0)), 0.0)
                low = jnp.where(rows > cols, beta * ratio * kk, 0.0)
                xs.append(
                    jnp.where(rows == cols, 1.0, jnp.where(rows // 2 == cols // 2, -low, 0.0)).astype(BF16)
                )
                lows.append(low.astype(BF16))
                growth = jnp.exp(cc)
                end = cr[:, tokens - 1 : tokens]
                tail = (jnp.exp(end - cc) * kn).astype(BF16)
                vv = v_ref[:, pl.ds(pl.multiple_of(head * DV, DV), DV)].astype(F32)
                rhs = jnp.concatenate([beta * vv, (beta * growth) * kn], axis=1).astype(BF16)
                uses.append((head, rhs, tail, (qk * ratio).astype(BF16), growth * qn, jnp.exp(end)))
        size = 2
        while size < tokens:
            shift = size.bit_length()
            mask = ((rows >> shift) == (cols >> shift)) & ((rows >> (shift - 1)) != (cols >> (shift - 1)))
            zero = jnp.zeros((tokens, tokens), BF16)
            ys = [dot_nn(jnp.where(mask, low, zero), x).astype(BF16) for low, x in zip(lows, xs)]
            xs = [(x.astype(F32) - dot_nn(x, y)).astype(BF16) for x, y in zip(xs, ys)]
            size *= 2
        for x, (head, rhs, tail, inner, grown, end) in zip(xs, uses):
            uw = dot_nn(x, rhs).astype(BF16)
            both = dot_tn(tail, uw)
            add_ref[head] = both[:, :DV]
            map_ref[head] = both[:, DV:].astype(BF16)
            growth_ref[head] = jnp.broadcast_to(end, (8, DV))
            core = dot_nn(inner, uw)
            core_add_ref[head] = core[:, :DV]
            core_map_ref[head] = (grown - core[:, DV:]).astype(BF16)

            @pl.when(ctx == 0)
            def first_state():
                state_out_ref[head] = both[:, :DV].astype(BF16)
                state_in_ref[head] = jnp.zeros((DK, DV), BF16)

        @pl.when(ctx == 0)
        def first_send():
            chain_copy(group).start()

    def finish_group(group):
        @pl.when(ctx > 0)
        def receive():
            chain_copy(group).wait_recv()

        @pl.when((ctx > 0) & (ctx < last))
        def forward():
            for step in range(HEADS_STEP):
                head = group * HEADS_STEP + step
                state = state_in_ref[head]
                grown = growth_ref[head][0:1, :] * state.astype(F32)
                state_out_ref[head] = (grown - dot_nn(map_ref[head], state) + add_ref[head]).astype(BF16)
            chain_copy(group).start()

        pieces = []
        for step in range(HEADS_STEP):
            head = group * HEADS_STEP + step
            core = core_add_ref[head] + dot_nn(core_map_ref[head], state_in_ref[head])
            scale = lax.rsqrt(jnp.mean(core * core, axis=-1, keepdims=True) + 1e-06)
            zz = z_ref[:, pl.ds(pl.multiple_of(head * DV, DV), DV)].astype(F32)
            act = zz / (1.0 + jnp.exp(-zz))
            pieces.append((core * scale * head_gain_ref[...] * act).astype(BF16))
        gated = jnp.concatenate(pieces, axis=1)
        span = HEADS_STEP * DV
        acc_ref[...] += dot_nn(gated, proj_ref[pl.ds(pl.multiple_of(group * span, span), span), :])

    def local_step(group, carry):
        local_group(group)

        return carry

    lax.fori_loop(0, groups, local_step, 0)

    def early_own(u, carry):
        early_piece(u)
        return carry

    def early_ahead(u, carry):
        piece_ahead(u)
        return carry

    before = jnp.maximum(depth, 1)
    lax.fori_loop(0, before, early_own, 0)
    for load in loads[5:12]:
        load.wait()
    acc_ref[...] = hidden_ref[...].astype(F32)

    def finish_step(group, carry):
        finish_group(group)
        lax.fori_loop(
            jnp.where(group == 0, before, depth + 1 + group // 2), depth + 1 + (group + 1) // 2, early_own, 0
        )
        lax.fori_loop(
            jnp.where(group < 2, 0, depth),
            jnp.where(group == 0, 0, jnp.where(group < groups - 1, depth, depth + 1)),
            early_ahead,
            0,
        )
        return carry

    lax.fori_loop(0, groups, finish_step, 0)

    def late_start(u, carry):
        ring(0, ctx, u, along(2)).start()
        return carry

    lax.fori_loop(jnp.where(top, depth + 3, depth), depth + 3, late_start, 0)
    mixed = acc_ref[...]
    scale = lax.rsqrt(jnp.mean(mixed * mixed, axis=-1, keepdims=True) + 1e-06)
    normed = (mixed * scale * moe_gain_ref[...]).astype(BF16)
    logits = dot_nt(router_ref[...], normed)
    place = lax.broadcasted_iota(jnp.int32, (experts, tokens), 0)
    chosen = place == ids_ref[0]
    for k in range(1, ids_ref.shape[0]):
        chosen = chosen | (place == ids_ref[k])
    sigmas = jnp.where(chosen, 1.0 / (1.0 + jnp.exp(-logits)), 0.0)
    gates = (sigmas / jnp.sum(sigmas, axis=0, keepdims=True)).T
    high = gates.astype(BF16)
    lows = (gates - high.astype(F32)).astype(BF16)

    quarter = half // 2

    def own(n):
        return 2 + n + 2 * (n // 2)

    def cross(n):
        return lax.rem(n + 4, 6)

    def at(slot, part, piece):
        return pl.ds(pl.multiple_of(slot * tokens + part * half + piece * quarter, quarter), quarter)

    home = pl.ds(7 * tokens, tokens)
    rows_ref[home, :width] = normed
    rows_ref[home, width:] = jnp.concatenate(
        [high, lows, jnp.zeros((tokens, 128 - 2 * experts), BF16)], axis=1
    )

    def remote(src, dst, send, recv, target):
        return pltpu.make_async_remote_copy(
            src_ref=src, dst_ref=dst, send_sem=send, recv_sem=recv, device_id={"dp": target}, device_id_type=MESH
        )

    def gather_y(part, k, piece):
        n = (part * 3 + k) * 2 + piece
        return remote(
            rows_ref.at[at(own(lax.rem(k + 3, 4)), part, piece)], rows_ref.at[at(own(k), part, piece)],
            gy_send.at[n], gy_recv.at[n], (down, up)[part],
        )

    def gather_x(part, k, piece):
        n = (part * 4 + k) * 2 + piece
        return remote(
            rows_ref.at[at(own(lax.rem(k + 3, 4)), part, piece)], rows_ref.at[at(cross(lax.rem(k + 3, 4)), part, piece)],
            gx_send.at[n], gx_recv.at[n], (right, left)[part],
        )

    def sum_x(part, n, piece):
        slot = (part * 4 + n) * 2 + piece
        return remote(
            part_ref.at[at(cross(n), part, piece)], xsum_ref.at[at(n, part, piece)],
            sx_send.at[slot], sx_recv.at[slot], (left, right)[part],
        )

    def sum_y(part, n, piece):
        slot = (part * 3 + n) * 2 + piece
        return remote(
            part_ref.at[at(own(n), part, piece)], ysum_ref.at[at(n, part, piece)],
            sy_send.at[slot], sy_recv.at[slot], (down, up)[part],
        )

    def send_rows(k, piece):
        for part in range(2):
            if isinstance(k, int):
                gather_y(part, k, piece).start()
            else:
                pl.when(k < 3)(gather_y(part, k, piece).start)
            gather_x(part, k, piece).start()

    def take_rows(k):
        for piece in range(2):
            for part in range(2):
                gather_y(part, k - 1, piece).wait_recv()
            send_rows(k, piece)

    def take_cross(k):
        for piece in range(2):
            for part in range(2):
                gather_x(part, k, piece).wait_recv()

    def ffn(start, count, in_ref, down_ref, first, number, owner, add):
        block = pl.ds(start if isinstance(start, int) else pl.multiple_of(start, tokens), count)
        hidden = down_ref.shape[0] // local

        def up_tile(n, carry):
            e = first + n
            x = rows_ref[block, :width]
            base = e * 2 * width
            base = base if isinstance(base, int) else pl.multiple_of(base, width)
            gate_part = dot_nn(x, in_ref[pl.ds(base, width), :])
            up_part = dot_nn(x, in_ref[pl.ds(base + width, width), :])
            extra = rows_ref[block, width:].astype(F32)
            lane = lax.broadcasted_iota(jnp.int32, extra.shape, 1)
            mine = owner * local + e
            gate = jnp.sum(jnp.where((lane == mine) | (lane == mine + experts), extra, 0.0), axis=1, keepdims=True)
            inner = gate_part / (1.0 + jnp.exp(-gate_part)) * up_part * gate
            lanes = pl.ds(0 if number == 1 else pl.multiple_of(n * hidden, hidden), hidden)
            inner_ref[pl.ds(0, count), lanes] = inner.astype(BF16)
            return carry

        if number == 1:
            up_tile(0, 0)
        else:
            lax.fori_loop(0, number, up_tile, 0)
        wide = width // 2

        def down_tile(n, carry):
            lanes = pl.ds(pl.multiple_of(n * wide, wide), wide)
            total = dot_nn(
                inner_ref[pl.ds(0, count), : number * hidden],
                down_ref[pl.ds(first * hidden, number * hidden), lanes],
            )
            if add:
                total += part_ref[block, lanes].astype(F32)
            part_ref[block, lanes] = total.astype(BF16)
            return carry

        lax.fori_loop(0, 2, down_tile, 0)

    def near_experts(slot, count):
        ffn(slot * tokens, count * tokens, win_ref, wdown_ref, 0, local, dp, False)

    def far_expert(slot, e):
        ffn(slot * tokens, 2 * tokens, far_in_ref, far_down_ref, e, 1, partner, True)

    send_rows(0, 0)
    send_rows(0, 1)
    greeting = (depth + 4, jnp.minimum(depth + 2, 4), 1, 0)
    weights(early, greeting)
    for load in loads[12:]:
        load.wait()
    near_experts(7, 1)
    weights(greeting, stages[0])
    take_rows(1)
    take_cross(0)

    def near_step(n, carry):
        near_experts(1 + 2 * n, 2)

        @pl.when(n < 2)
        def more():
            take_rows(n + 2)
            weights(pick(n, stages[0:2]), pick(n, stages[1:3]))
            take_cross(n + 1)

        return carry

    lax.fori_loop(0, 3, near_step, 0)
    weights(stages[2], stages[3])
    for u in range(UNITS // 2):
        share_recv_all(u)

    def far_first(n, carry):
        far_expert(lax.rem(4 + 2 * n, 8) - 2 * (n // 2) + 4 * (n // 2) - 4 * (n // 3), 0)

        @pl.when(n == 1)
        def tail_rows():
            take_cross(3)
            near_experts(0, 1)

        @pl.when(n < 3)
        def more():
            weights(pick(n, stages[3:6]), pick(n, stages[4:7]))

        return carry

    lax.fori_loop(0, 4, far_first, 0)
    weights(stages[6], stages[7])
    for u in range(UNITS // 2, UNITS):
        share_recv_all(u)

    def far_cross(n, carry):
        far_expert(cross(2 * n), 1)
        for m in range(2):
            for piece in range(2):
                for part in range(2):
                    sum_x(part, 2 * n + m, piece).start()
        return carry

    lax.fori_loop(0, 2, far_cross, 0)

    def far_own(n, carry):
        far_expert(own(2 * n), 1)
        return carry

    lax.fori_loop(0, 2, far_own, 0)

    def collect(n, carry):
        for piece in range(2):
            for part in range(2):
                sum_x(part, n, piece).wait_recv()
                spot = at(own(n), part, piece)
                both = part_ref[spot, :].astype(F32) + xsum_ref[at(n, part, piece), :].astype(F32)

                @pl.when(n == 0)
                def begin():
                    part_ref[spot, :] = both.astype(BF16)

                @pl.when(n > 0)
                def more():
                    sum_y(part, n - 1, piece).wait_recv()
                    total = both + ysum_ref[at(n - 1, part, piece), :].astype(F32)

                    @pl.when(n < 3)
                    def keep():
                        part_ref[spot, :] = total.astype(BF16)

                    @pl.when(n == 3)
                    def finish():
                        span = pl.ds(part * half + piece * quarter, quarter)
                        out_ref[span, :] = (acc_ref[span, :] + total).astype(BF16)

                @pl.when(n < 3)
                def onward():
                    sum_y(part, n, piece).start()

        return carry

    lax.fori_loop(0, 4, collect, 0)

    for part in range(2):
        for piece in range(2):
            for k in range(4):
                gather_x(part, k, piece).wait_send()
                sum_x(part, k, piece).wait_send()
            for k in range(3):
                gather_y(part, k, piece).wait_send()
                sum_y(part, k, piece).wait_send()
    for u in range(UNITS):
        fetch(u).wait_send()
        ring(0, ctx, u, along(2)).wait_send()
        ring(1, ctx, u, along(-2)).wait_send()
        ring(2, along(-2) if u % 2 == 0 else along(2), u, along(2)).wait_send()
        for lane, step in enumerate((0, -2, 2, 4)):
            share(lane, along(step), u).wait_send()

    @pl.when(ctx < last)
    def drain():
        for group in range(groups):
            chain_copy(group).wait_send()


def layer(q, k, v, z, beta, decay, hidden, head_gain, moe_gain, router, ids, proj, win, wdown):
    tokens, width = hidden.shape
    heads = v.shape[1] // DV
    args = (q, k, v, z, beta, decay, hidden, head_gain, moe_gain, router, ids, proj, win, wdown)
    hbm = pl.BlockSpec(memory_space=pltpu.HBM)
    dma = pltpu.SemaphoreType.DMA
    return pl.pallas_call(
        layer_kernel,
        out_shape=jax.ShapeDtypeStruct((tokens, width), BF16),
        in_specs=[hbm] * len(args),
        out_specs=pl.BlockSpec(memory_space=pltpu.VMEM),
        scratch_shapes=[pltpu.VMEM(arg.shape, arg.dtype) for arg in args]
        + [
            pltpu.VMEM(win.shape, BF16),
            pltpu.VMEM(wdown.shape, BF16),
            pltpu.VMEM((heads, tokens), F32),
            pltpu.VMEM((heads, DK, DV), F32),
            pltpu.VMEM((heads, DK, DV), BF16),
            pltpu.VMEM((heads, 8, DV), F32),
            pltpu.VMEM((heads, tokens, DV), F32),
            pltpu.VMEM((heads, tokens, DV), BF16),
            pltpu.VMEM((heads, DK, DV), BF16),
            pltpu.VMEM((heads, DK, DV), BF16),
            pltpu.VMEM((tokens, width), F32),
            pltpu.VMEM((8 * tokens, width + 128), BF16),
            pltpu.VMEM((8 * tokens, width), BF16),
            pltpu.VMEM((4 * tokens, width), BF16),
            pltpu.VMEM((3 * tokens, width), BF16),
            pltpu.VMEM((2 * tokens, wdown.shape[0]), BF16),
            dma((len(args),)),
            dma((heads // HEADS_STEP,)),
            dma((heads // HEADS_STEP,)),
            dma((2 * UNITS,)),
            dma((2 * UNITS,)),
            dma((6 * UNITS,)),
            dma((6 * UNITS,)),
            dma((8 * UNITS,)),
            dma((8 * UNITS,)),
            dma((16,)),
            dma((16,)),
            dma((12,)),
            dma((12,)),
            dma((16,)),
            dma((16,)),
            dma((12,)),
            dma((12,)),
        ],
        compiler_params=pltpu.CompilerParams(
            collective_id=0, has_side_effects=True, vmem_limit_bytes=62 * 1024 * 1024
        ),
    )(*args)


def per_device(
    hidden_in,
    queries,
    key_vectors,
    value_rows,
    out_gate,
    beta_rate,
    log_decay,
    head_gain,
    out_proj,
    moe_gain,
    router,
    expert_ids,
    expert_in,
    expert_down,
):
    return layer(
        queries[0],
        key_vectors[0],
        value_rows[0],
        out_gate[0],
        beta_rate[0].T,
        log_decay[0].T,
        hidden_in[0],
        head_gain[None],
        moe_gain[None],
        router.T,
        expert_ids.transpose(2, 0, 1),
        out_proj,
        expert_in.reshape(-1, expert_in.shape[-1]),
        expert_down.reshape(-1, expert_down.shape[-1]),
    )[None]


def solution(mesh):
    in_specs = (
        P("dp", "ctx", None),
        P("dp", "ctx", None),
        P("dp", "ctx", None),
        P("dp", "ctx", None),
        P("dp", "ctx", None),
        P("dp", "ctx", None),
        P("dp", "ctx", None),
        P(),
        P(),
        P(),
        P(),
        P("dp", "ctx", None),
        P("dp", None, None, None),
        P("dp", None, None),
    )
    out_specs = P("dp", "ctx", None)
    return jax.shard_map(
        per_device, mesh=mesh, in_specs=in_specs, out_specs=out_specs, check_vma=False
    )
```

```python
import functools

import jax
import jax.numpy as jnp
from jax import lax
from jax.experimental import pallas as pl
from jax.experimental.pallas import tpu as pltpu
from jax.sharding import PartitionSpec as P

DK = 128
DV = 128
SIDE = 4
HIGHEST = lax.Precision.HIGHEST
F32 = jnp.float32
BF16 = jnp.bfloat16


def dot_nn(a, b):
    return lax.dot_general(a, b, (((1,), (0,)), ((), ())), preferred_element_type=F32)


def dot_nt(a, b):
    return lax.dot_general(a, b, (((1,), (1,)), ((), ())), preferred_element_type=F32)


def dot_tn(a, b):
    return lax.dot_general(a, b, (((0,), (0,)), ((), ())), preferred_element_type=F32)


def unit_rows(matrix):
    return matrix * lax.rsqrt(jnp.sum(matrix * matrix, axis=-1, keepdims=True) + 1e-06)


HEADS_STEP = 4
UNITS = 8
MESH = pl.DeviceIdType.MESH


def layer_kernel(
    q_hbm,
    k_hbm,
    v_hbm,
    z_hbm,
    beta_hbm,
    decay_hbm,
    hidden_hbm,
    head_gain_hbm,
    moe_gain_hbm,
    router_hbm,
    ids_hbm,
    proj_hbm,
    win_hbm,
    wdown_hbm,
    out_ref,
    q_ref,
    k_ref,
    v_ref,
    z_ref,
    beta_ref,
    decay_ref,
    hidden_ref,
    head_gain_ref,
    moe_gain_ref,
    router_ref,
    ids_ref,
    proj_ref,
    win_ref,
    wdown_ref,
    far_in_ref,
    far_down_ref,
    cum_ref,
    add_ref,
    map_ref,
    growth_ref,
    core_add_ref,
    core_map_ref,
    state_in_ref,
    state_out_ref,
    acc_ref,
    rows_ref,
    part_ref,
    xsum_ref,
    ysum_ref,
    inner_ref,
    in_sem,
    chain_send,
    chain_recv,
    fetch_send,
    fetch_recv,
    ring_send,
    ring_recv,
    share_send,
    share_recv,
    gx_send,
    gx_recv,
    gy_send,
    gy_recv,
    sx_send,
    sx_recv,
    sy_send,
    sy_recv,
):
    ctx = lax.axis_index("ctx")
    shards = lax.axis_size("ctx")
    last = shards - 1
    dp = lax.axis_index("dp")
    row, col = dp // SIDE, lax.rem(dp, SIDE)
    tokens, width = hidden_ref.shape
    heads = v_ref.shape[1] // DV
    groups = heads // HEADS_STEP
    experts = router_ref.shape[0]
    local = experts // lax.axis_size("dp")
    half = tokens // 2

    def beside(dr, dc):
        return lax.rem(row + dr + SIDE, SIDE) * SIDE + lax.rem(col + dc + SIDE, SIDE)

    def along(step):
        return lax.rem(ctx + step + shards, shards)

    right, left, down, up = beside(0, 1), beside(0, -1), beside(1, 0), beside(-1, 0)
    partner = beside(0, 2)
    sibling = ctx + 1 - 2 * lax.rem(ctx, 2)

    barrier = pltpu.get_barrier_semaphore()
    for target in (right, left, down, up, partner):
        pl.semaphore_signal(barrier, inc=1, device_id={"dp": target}, device_id_type=MESH)
    for step in (1, -1, 2, -2):
        pl.semaphore_signal(barrier, inc=1, device_id={"ctx": along(step)}, device_id_type=MESH)

    loads = [
        pltpu.make_async_copy(src, dst, in_sem.at[n])
        for n, (src, dst) in enumerate(
            (
                (decay_hbm, decay_ref),
                (beta_hbm, beta_ref),
                (k_hbm, k_ref),
                (q_hbm, q_ref),
                (v_hbm, v_ref),
                (z_hbm, z_ref),
                (hidden_hbm, hidden_ref),
                (head_gain_hbm, head_gain_ref),
                (moe_gain_hbm, moe_gain_ref),
                (router_hbm, router_ref),
                (ids_hbm, ids_ref),
                (proj_hbm, proj_ref),
                (win_hbm, win_ref),
                (wdown_hbm, wdown_ref),
            )
        )
    ]
    for load in loads[:11]:
        load.start()

    in_span = win_hbm.shape[0] // (UNITS * shards)
    down_span = wdown_hbm.shape[0] // (UNITS * shards)

    def weight_spans(owner, u):
        n = u * shards + owner
        return (
            pl.ds(pl.multiple_of(n * in_span, in_span), in_span),
            pl.ds(pl.multiple_of(n * down_span, down_span), down_span),
        )

    class Both:
        def __init__(self, src, owner, u, send, recv, slot, target):
            spans = weight_spans(owner, u)
            self.copies = [
                pltpu.make_async_remote_copy(
                    src_ref=ref.at[span],
                    dst_ref=dst.at[span],
                    send_sem=send.at[slot * 2 + n],
                    recv_sem=recv.at[slot * 2 + n],
                    device_id=target,
                    device_id_type=MESH,
                )
                for n, (ref, dst, span) in enumerate(zip(src, (far_in_ref, far_down_ref), spans))
            ]

        def start(self):
            for copy in self.copies:
                copy.start()

        def wait_recv(self):
            for copy in self.copies:
                copy.wait_recv()

        def wait_send(self):
            for copy in self.copies:
                copy.wait_send()

    far = (far_in_ref, far_down_ref)

    def fetch(u):
        return Both((win_hbm, wdown_hbm), ctx, u, fetch_send, fetch_recv, u, {"dp": partner})

    def ring(lane, owner, u, target):
        return Both(far, owner, u, ring_send, ring_recv, lane * UNITS + u, {"ctx": target})

    def share(lane, owner, u):
        return Both(far, owner, u, share_send, share_recv, lane * UNITS + u, {"ctx": sibling})

    depth = ctx // 2
    top = depth == last // 2

    def early_piece(u):
        fetch(u).wait_recv()
        ring(1, ctx, u, along(-2)).start()
        share(0, ctx, u).start()
        pl.when(top | (u < depth))(ring(0, ctx, u, along(2)).start)

    def own_piece(u):
        fetch(u).wait_recv()
        ring(1, ctx, u, along(-2)).start()
        share(0, ctx, u).start()
        ring(0, ctx, u, along(2)).start()

    def piece_ahead(u):
        ahead = along(2)
        ring(1, ahead, u, along(-2)).wait_recv()

        @pl.when(lax.rem(u, 4) > 0)
        def onward():
            ring(2, ahead, u, along(-2)).start()

        share(2, ahead, u).start()

    def piece_behind(u):
        behind = along(-2)
        ring(0, behind, u, along(2)).wait_recv()

        @pl.when(lax.rem(u, 4) == 0)
        def onward():
            ring(2, behind, u, along(2)).start()

        share(1, behind, u).start()

    def piece_opposite(u):
        ring(2, along(4), u, along(2)).wait_recv()
        share(3, along(4), u).start()

    kinds = (own_piece, piece_ahead, piece_behind, piece_opposite)

    def weights(since, until):
        for move, low, high in zip(kinds, since, until):
            if low is not high:

                def one(u, carry, move=move):
                    move(u)
                    return carry

                lax.fori_loop(low, high, one, 0)

    odd = (depth + 1) // 2
    early = (depth + 3, depth + 1, 0, 0)
    stages = (
        (depth + 5, jnp.minimum(depth + 3, 5), 2, 0),
        (UNITS, 4 + odd, 4, 1),
        (UNITS, 6 + odd, 6, 4),
        (UNITS, UNITS, 7, 5),
        (UNITS, UNITS, UNITS, 6),
        (UNITS, UNITS, UNITS, UNITS),
        (UNITS, UNITS, UNITS, UNITS),
        (UNITS, UNITS, UNITS, UNITS),
    )

    def pick(n, options):
        return tuple(
            functools.reduce(lambda other, m: jnp.where(n == m, options[m][kind], other), range(1, len(options)), options[0][kind])
            for kind in range(4)
        )

    def share_recv_all(u):
        for lane, step in enumerate((0, -2, 2, 4)):
            share(lane, lax.rem(sibling + step + shards, shards), u).wait_recv()

    pl.semaphore_wait(barrier, 9)
    for u in range(UNITS):
        fetch(u).start()
    for load in loads[11:]:
        load.start()
    for load in loads[:5]:
        load.wait()

    rows = lax.broadcasted_iota(jnp.int32, (tokens, tokens), 0)
    cols = lax.broadcasted_iota(jnp.int32, (tokens, tokens), 1)
    lower = rows >= cols
    head_lane = lax.broadcasted_iota(jnp.int32, (tokens, heads), 1)
    cum_rows = lax.dot_general(
        decay_ref[...], (rows <= cols).astype(F32), (((1,), (0,)), ((), ())),
        preferred_element_type=F32, precision=HIGHEST,
    )
    cum_ref[...] = cum_rows
    cumul = cum_rows.T
    betas = beta_ref[...].T

    def chain_copy(group):
        part = pl.ds(group * HEADS_STEP, HEADS_STEP)
        return pltpu.make_async_remote_copy(
            src_ref=state_out_ref.at[part],
            dst_ref=state_in_ref.at[part],
            send_sem=chain_send.at[group],
            recv_sem=chain_recv.at[group],
            device_id={"ctx": along(1)},
            device_id_type=MESH,
        )

    def local_group(group):
        xs, lows, uses = [], [], []
        for pair in range(HEADS_STEP // 2):
            lanes = pl.ds(pl.multiple_of((group * (HEADS_STEP // 2) + pair) * DK, DK), DK)
            kn = unit_rows(k_ref[:, lanes].astype(F32))
            qn = unit_rows(q_ref[:, lanes].astype(F32))
            knb, qnb = kn.astype(BF16), qn.astype(BF16)
            kk, qk = dot_nt(knb, knb), dot_nt(qnb, knb)
            for other in range(2):
                head = group * HEADS_STEP + pair * 2 + other
                pick = head_lane == head
                beta = jnp.sum(jnp.where(pick, betas, 0.0), axis=1, keepdims=True)
                cc = jnp.sum(jnp.where(pick, cumul, 0.0), axis=1, keepdims=True)
                cr = cum_ref[pl.ds(head, 1), :]
                ratio = jnp.where(lower, jnp.exp(jnp.minimum(cc - cr, 0.0)), 0.0)
                low = jnp.where(rows > cols, beta * ratio * kk, 0.0)
                xs.append(
                    jnp.where(rows == cols, 1.0, jnp.where(rows // 2 == cols // 2, -low, 0.0)).astype(BF16)
                )
                lows.append(low.astype(BF16))
                growth = jnp.exp(cc)
                end = cr[:, tokens - 1 : tokens]
                tail = (jnp.exp(end - cc) * kn).astype(BF16)
                vv = v_ref[:, pl.ds(pl.multiple_of(head * DV, DV), DV)].astype(F32)
                rhs = jnp.concatenate([beta * vv, (beta * growth) * kn], axis=1).astype(BF16)
                uses.append((head, rhs, tail, (qk * ratio).astype(BF16), growth * qn, jnp.exp(end)))
        size = 2
        while size < tokens:
            shift = size.bit_length()
            mask = ((rows >> shift) == (cols >> shift)) & ((rows >> (shift - 1)) != (cols >> (shift - 1)))
            zero = jnp.zeros((tokens, tokens), BF16)
            ys = [dot_nn(jnp.where(mask, low, zero), x).astype(BF16) for low, x in zip(lows, xs)]
            xs = [(x.astype(F32) - dot_nn(x, y)).astype(BF16) for x, y in zip(xs, ys)]
            size *= 2
        for x, (head, rhs, tail, inner, grown, end) in zip(xs, uses):
            uw = dot_nn(x, rhs).astype(BF16)
            both = dot_tn(tail, uw)
            add_ref[head] = both[:, :DV]
            map_ref[head] = both[:, DV:].astype(BF16)
            growth_ref[head] = jnp.broadcast_to(end, (8, DV))
            core = dot_nn(inner, uw)
            core_add_ref[head] = core[:, :DV]
            core_map_ref[head] = (grown - core[:, DV:]).astype(BF16)

            @pl.when(ctx == 0)
            def first_state():
                state_out_ref[head] = both[:, :DV].astype(BF16)
                state_in_ref[head] = jnp.zeros((DK, DV), BF16)

        @pl.when(ctx == 0)
        def first_send():
            chain_copy(group).start()

    def finish_group(group):
        @pl.when(ctx > 0)
        def receive():
            chain_copy(group).wait_recv()

        @pl.when((ctx > 0) & (ctx < last))
        def forward():
            for step in range(HEADS_STEP):
                head = group * HEADS_STEP + step
                state = state_in_ref[head]
                grown = growth_ref[head][0:1, :] * state.astype(F32)
                state_out_ref[head] = (grown - dot_nn(map_ref[head], state) + add_ref[head]).astype(BF16)
            chain_copy(group).start()

        pieces = []
        for step in range(HEADS_STEP):
            head = group * HEADS_STEP + step
            core = core_add_ref[head] + dot_nn(core_map_ref[head], state_in_ref[head])
            scale = lax.rsqrt(jnp.mean(core * core, axis=-1, keepdims=True) + 1e-06)
            zz = z_ref[:, pl.ds(pl.multiple_of(head * DV, DV), DV)].astype(F32)
            act = zz / (1.0 + jnp.exp(-zz))
            pieces.append((core * scale * head_gain_ref[...] * act).astype(BF16))
        gated = jnp.concatenate(pieces, axis=1)
        span = HEADS_STEP * DV
        acc_ref[...] += dot_nn(gated, proj_ref[pl.ds(pl.multiple_of(group * span, span), span), :])

    def local_step(group, carry):
        local_group(group)

        return carry

    lax.fori_loop(0, groups, local_step, 0)

    def early_own(u, carry):
        early_piece(u)
        return carry

    def early_ahead(u, carry):
        piece_ahead(u)
        return carry

    before = jnp.maximum(depth, 1)
    lax.fori_loop(0, before, early_own, 0)
    for load in loads[5:12]:
        load.wait()
    acc_ref[...] = hidden_ref[...].astype(F32)

    def finish_step(group, carry):
        finish_group(group)
        lax.fori_loop(
            jnp.where(group == 0, before, depth + 1 + group // 2), depth + 1 + (group + 1) // 2, early_own, 0
        )
        lax.fori_loop(
            jnp.where(group < 2, 0, depth),
            jnp.where(group == 0, 0, jnp.where(group < groups - 1, depth, depth + 1)),
            early_ahead,
            0,
        )
        return carry

    lax.fori_loop(0, groups, finish_step, 0)

    def late_start(u, carry):
        ring(0, ctx, u, along(2)).start()
        return carry

    lax.fori_loop(jnp.where(top, depth + 3, depth), depth + 3, late_start, 0)
    mixed = acc_ref[...]
    scale = lax.rsqrt(jnp.mean(mixed * mixed, axis=-1, keepdims=True) + 1e-06)
    normed = (mixed * scale * moe_gain_ref[...]).astype(BF16)
    logits = dot_nt(router_ref[...], normed)
    place = lax.broadcasted_iota(jnp.int32, (experts, tokens), 0)
    chosen = place == ids_ref[0]
    for k in range(1, ids_ref.shape[0]):
        chosen = chosen | (place == ids_ref[k])
    sigmas = jnp.where(chosen, 1.0 / (1.0 + jnp.exp(-logits)), 0.0)
    gates = (sigmas / jnp.sum(sigmas, axis=0, keepdims=True)).T
    high = gates.astype(BF16)
    lows = (gates - high.astype(F32)).astype(BF16)

    quarter = half // 2

    def own(n):
        return 2 + n + 2 * (n // 2)

    def cross(n):
        return lax.rem(n + 4, 6)

    def at(slot, part, piece):
        return pl.ds(pl.multiple_of(slot * tokens + part * half + piece * quarter, quarter), quarter)

    home = pl.ds(7 * tokens, tokens)
    rows_ref[home, :width] = normed
    rows_ref[home, width:] = jnp.concatenate(
        [high, lows, jnp.zeros((tokens, 128 - 2 * experts), BF16)], axis=1
    )

    def remote(src, dst, send, recv, target):
        return pltpu.make_async_remote_copy(
            src_ref=src, dst_ref=dst, send_sem=send, recv_sem=recv, device_id={"dp": target}, device_id_type=MESH
        )

    def gather_y(part, k, piece):
        n = (part * 3 + k) * 2 + piece
        return remote(
            rows_ref.at[at(own(lax.rem(k + 3, 4)), part, piece)], rows_ref.at[at(own(k), part, piece)],
            gy_send.at[n], gy_recv.at[n], (down, up)[part],
        )

    def gather_x(part, k, piece):
        n = (part * 4 + k) * 2 + piece
        return remote(
            rows_ref.at[at(own(lax.rem(k + 3, 4)), part, piece)], rows_ref.at[at(cross(lax.rem(k + 3, 4)), part, piece)],
            gx_send.at[n], gx_recv.at[n], (right, left)[part],
        )

    def sum_x(part, n, piece):
        slot = (part * 4 + n) * 2 + piece
        return remote(
            part_ref.at[at(cross(n), part, piece)], xsum_ref.at[at(n, part, piece)],
            sx_send.at[slot], sx_recv.at[slot], (left, right)[part],
        )

    def sum_y(part, n, piece):
        slot = (part * 3 + n) * 2 + piece
        return remote(
            part_ref.at[at(own(n), part, piece)], ysum_ref.at[at(n, part, piece)],
            sy_send.at[slot], sy_recv.at[slot], (down, up)[part],
        )

    def send_rows(k, piece):
        for part in range(2):
            if isinstance(k, int):
                gather_y(part, k, piece).start()
            else:
                pl.when(k < 3)(gather_y(part, k, piece).start)
            gather_x(part, k, piece).start()

    def take_rows(k):
        for piece in range(2):
            for part in range(2):
                gather_y(part, k - 1, piece).wait_recv()
            send_rows(k, piece)

    def take_cross(k):
        for piece in range(2):
            for part in range(2):
                gather_x(part, k, piece).wait_recv()

    def ffn(start, count, in_ref, down_ref, first, number, owner, add):
        block = pl.ds(start if isinstance(start, int) else pl.multiple_of(start, tokens), count)
        hidden = down_ref.shape[0] // local

        def up_tile(n, carry):
            e = first + n
            x = rows_ref[block, :width]
            base = e * 2 * width
            base = base if isinstance(base, int) else pl.multiple_of(base, width)
            gate_part = dot_nn(x, in_ref[pl.ds(base, width), :])
            up_part = dot_nn(x, in_ref[pl.ds(base + width, width), :])
            extra = rows_ref[block, width:].astype(F32)
            lane = lax.broadcasted_iota(jnp.int32, extra.shape, 1)
            mine = owner * local + e
            gate = jnp.sum(jnp.where((lane == mine) | (lane == mine + experts), extra, 0.0), axis=1, keepdims=True)
            inner = gate_part / (1.0 + jnp.exp(-gate_part)) * up_part * gate
            lanes = pl.ds(0 if number == 1 else pl.multiple_of(n * hidden, hidden), hidden)
            inner_ref[pl.ds(0, count), lanes] = inner.astype(BF16)
            return carry

        if number == 1:
            up_tile(0, 0)
        else:
            lax.fori_loop(0, number, up_tile, 0)
        wide = width // 2

        def down_tile(n, carry):
            lanes = pl.ds(pl.multiple_of(n * wide, wide), wide)
            total = dot_nn(
                inner_ref[pl.ds(0, count), : number * hidden],
                down_ref[pl.ds(first * hidden, number * hidden), lanes],
            )
            if add:
                total += part_ref[block, lanes].astype(F32)
            part_ref[block, lanes] = total.astype(BF16)
            return carry

        lax.fori_loop(0, 2, down_tile, 0)

    def near_experts(slot, count):
        ffn(slot * tokens, count * tokens, win_ref, wdown_ref, 0, local, dp, False)

    def far_expert(slot, e):
        ffn(slot * tokens, 2 * tokens, far_in_ref, far_down_ref, e, 1, partner, True)

    send_rows(0, 0)
    send_rows(0, 1)
    greeting = (depth + 4, depth + 1, 1, 0)
    weights(early, greeting)
    for load in loads[12:]:
        load.wait()
    near_experts(7, 1)
    weights(greeting, stages[0])
    take_rows(1)
    take_cross(0)

    def near_step(n, carry):
        near_experts(1 + 2 * n, 2)

        @pl.when(n < 2)
        def more():
            take_rows(n + 2)
            weights(pick(n, stages[0:2]), pick(n, stages[1:3]))
            take_cross(n + 1)

        return carry

    lax.fori_loop(0, 3, near_step, 0)
    weights(stages[2], stages[3])
    for u in range(UNITS // 2):
        share_recv_all(u)

    def far_first(n, carry):
        far_expert(lax.rem(4 + 2 * n, 8) - 2 * (n // 2) + 4 * (n // 2) - 4 * (n // 3), 0)

        @pl.when(n == 1)
        def tail_rows():
            take_cross(3)
            near_experts(0, 1)

        @pl.when(n < 3)
        def more():
            weights(pick(n, stages[3:6]), pick(n, stages[4:7]))

        return carry

    lax.fori_loop(0, 4, far_first, 0)
    weights(stages[6], stages[7])
    for u in range(UNITS // 2, UNITS):
        share_recv_all(u)

    def far_cross(n, carry):
        far_expert(cross(2 * n), 1)
        for m in range(2):
            for piece in range(2):
                for part in range(2):
                    sum_x(part, 2 * n + m, piece).start()
        return carry

    lax.fori_loop(0, 2, far_cross, 0)

    def far_own(n, carry):
        far_expert(own(2 * n), 1)
        return carry

    lax.fori_loop(0, 2, far_own, 0)

    def collect(n, carry):
        for piece in range(2):
            for part in range(2):
                sum_x(part, n, piece).wait_recv()
                spot = at(own(n), part, piece)
                both = part_ref[spot, :].astype(F32) + xsum_ref[at(n, part, piece), :].astype(F32)

                @pl.when(n == 0)
                def begin():
                    part_ref[spot, :] = both.astype(BF16)

                @pl.when(n > 0)
                def more():
                    sum_y(part, n - 1, piece).wait_recv()
                    total = both + ysum_ref[at(n - 1, part, piece), :].astype(F32)

                    @pl.when(n < 3)
                    def keep():
                        part_ref[spot, :] = total.astype(BF16)

                    @pl.when(n == 3)
                    def finish():
                        span = pl.ds(part * half + piece * quarter, quarter)
                        out_ref[span, :] = (acc_ref[span, :] + total).astype(BF16)

                @pl.when(n < 3)
                def onward():
                    sum_y(part, n, piece).start()

        return carry

    lax.fori_loop(0, 4, collect, 0)

    for part in range(2):
        for piece in range(2):
            for k in range(4):
                gather_x(part, k, piece).wait_send()
                sum_x(part, k, piece).wait_send()
            for k in range(3):
                gather_y(part, k, piece).wait_send()
                sum_y(part, k, piece).wait_send()
    for u in range(UNITS):
        fetch(u).wait_send()
        ring(0, ctx, u, along(2)).wait_send()
        ring(1, ctx, u, along(-2)).wait_send()
        ring(2, along(-2) if u % 2 == 0 else along(2), u, along(2)).wait_send()
        for lane, step in enumerate((0, -2, 2, 4)):
            share(lane, along(step), u).wait_send()

    @pl.when(ctx < last)
    def drain():
        for group in range(groups):
            chain_copy(group).wait_send()


def layer(q, k, v, z, beta, decay, hidden, head_gain, moe_gain, router, ids, proj, win, wdown):
    tokens, width = hidden.shape
    heads = v.shape[1] // DV
    args = (q, k, v, z, beta, decay, hidden, head_gain, moe_gain, router, ids, proj, win, wdown)
    hbm = pl.BlockSpec(memory_space=pltpu.HBM)
    dma = pltpu.SemaphoreType.DMA
    return pl.pallas_call(
        layer_kernel,
        out_shape=jax.ShapeDtypeStruct((tokens, width), BF16),
        in_specs=[hbm] * len(args),
        out_specs=pl.BlockSpec(memory_space=pltpu.VMEM),
        scratch_shapes=[pltpu.VMEM(arg.shape, arg.dtype) for arg in args]
        + [
            pltpu.VMEM(win.shape, BF16),
            pltpu.VMEM(wdown.shape, BF16),
            pltpu.VMEM((heads, tokens), F32),
            pltpu.VMEM((heads, DK, DV), F32),
            pltpu.VMEM((heads, DK, DV), BF16),
            pltpu.VMEM((heads, 8, DV), F32),
            pltpu.VMEM((heads, tokens, DV), F32),
            pltpu.VMEM((heads, tokens, DV), BF16),
            pltpu.VMEM((heads, DK, DV), BF16),
            pltpu.VMEM((heads, DK, DV), BF16),
            pltpu.VMEM((tokens, width), F32),
            pltpu.VMEM((8 * tokens, width + 128), BF16),
            pltpu.VMEM((8 * tokens, width), BF16),
            pltpu.VMEM((4 * tokens, width), BF16),
            pltpu.VMEM((3 * tokens, width), BF16),
            pltpu.VMEM((2 * tokens, wdown.shape[0]), BF16),
            dma((len(args),)),
            dma((heads // HEADS_STEP,)),
            dma((heads // HEADS_STEP,)),
            dma((2 * UNITS,)),
            dma((2 * UNITS,)),
            dma((6 * UNITS,)),
            dma((6 * UNITS,)),
            dma((8 * UNITS,)),
            dma((8 * UNITS,)),
            dma((16,)),
            dma((16,)),
            dma((12,)),
            dma((12,)),
            dma((16,)),
            dma((16,)),
            dma((12,)),
            dma((12,)),
        ],
        compiler_params=pltpu.CompilerParams(
            collective_id=0, has_side_effects=True, vmem_limit_bytes=62 * 1024 * 1024
        ),
    )(*args)


def per_device(
    hidden_in,
    queries,
    key_vectors,
    value_rows,
    out_gate,
    beta_rate,
    log_decay,
    head_gain,
    out_proj,
    moe_gain,
    router,
    expert_ids,
    expert_in,
    expert_down,
):
    return layer(
        queries[0],
        key_vectors[0],
        value_rows[0],
        out_gate[0],
        beta_rate[0].T,
        log_decay[0].T,
        hidden_in[0],
        head_gain[None],
        moe_gain[None],
        router.T,
        expert_ids.transpose(2, 0, 1),
        out_proj,
        expert_in.reshape(-1, expert_in.shape[-1]),
        expert_down.reshape(-1, expert_down.shape[-1]),
    )[None]


def solution(mesh):
    in_specs = (
        P("dp", "ctx", None),
        P("dp", "ctx", None),
        P("dp", "ctx", None),
        P("dp", "ctx", None),
        P("dp", "ctx", None),
        P("dp", "ctx", None),
        P("dp", "ctx", None),
        P(),
        P(),
        P(),
        P(),
        P("dp", "ctx", None),
        P("dp", None, None, None),
        P("dp", None, None),
    )
    out_specs = P("dp", "ctx", None)
    return jax.shard_map(
        per_device, mesh=mesh, in_specs=in_specs, out_specs=out_specs, check_vma=False
    )
```
